128 devices in a mesh: node: 16 (over y, x_hi, core), local: 8 (over z, x_lo).
Axes of the slice: x: 4 (x_hi: 2, x_lo: 2; x = x_hi * 2 + x_lo), y: 4, z: 4, core: 2. Of those that a mesh axis runs over, the one named last changes fastest.
Arguments:
- tokens: bfloat16 [16384, 4096], P(('node', 'local')), may hold values from -8 to 8
- norm_gain: bfloat16 [4096], replicated, may hold values from 0.25 to 1.75
- routes: int32 [16384, 8], P(('node', 'local')), may hold values from 0 to 127, as said below
- route_gates: float32 [16384, 8], P(('node', 'local')), may hold values from 0.35 to 1
- placement: int32 [128], replicated, may hold values from 0 to 127, each once
- gate_weight: bfloat16 [128, 4096, 768], P(('node', 'local')), may hold values from -0.09375 to 0.09375
- up_weight: bfloat16 [128, 4096, 768], P(('node', 'local')), may hold values from -0.09375 to 0.09375
- down_weight: bfloat16 [128, 768, 4096], P(('node', 'local')), may hold values from -0.21875 to 0.21875
Outputs:
- moe_output: bfloat16 [16384, 4096], P(('node', 'local'))
The draws below stay inside these ranges and needn't reach their ends.
Inputs may be any that keep to these rules, and one draw needn't show every extreme that they name: `routes`: each token names 8 different experts. In every aligned block of 32 tokens of one device, each expert is named at most 3 times; at every block position some expert is named exactly 3 times by that block of every device.
All inputs are finite; a program needn't handle non-finite values.
Results may differ from the reference program's by a relative error of at most 0.0076.
Values may be sent and summed in bfloat16 or wider, within the bound.
A program may use at most 128 MiB of HBM per device.

```python
import math
import jax
import jax.numpy as jnp
from jax import lax

D = 4096
TOPK = 8
HID = 768
BLOCKS = 4
BLOCK_TOK = 32
TOKENS = 16384
EXPERTS = 128
CAP = 3


def draw_tokens(key, part):
    key = jax.random.fold_in(key, 5)
    first_key, second_key, third_key = jax.random.split(key, 3)
    basic = jax.random.normal(first_key, (TOKENS, D), jnp.float32)
    columns = jnp.exp(jax.random.uniform(second_key, (D,), jnp.float32, math.log(0.5), math.log(5.0)))
    row_scale = jnp.exp(jax.random.uniform(third_key, (TOKENS, 1), jnp.float32, math.log(0.5), math.log(2.0)))
    return jnp.clip(basic * columns[None, :] * row_scale, -8.0, 8.0).astype(jnp.bfloat16)


def draw_routes(key, part):
    key = jax.random.fold_in(key, 11)
    groups = TOKENS // BLOCK_TOK
    per_expert = BLOCK_TOK * TOPK // EXPERTS
    spare = CAP - per_expert
    hot_base = jax.random.fold_in(key, 7)
    expert_ids = jnp.arange(EXPERTS, dtype=jnp.int32)
    list_pos = jnp.arange(BLOCK_TOK * TOPK, dtype=jnp.int32)

    def one_block(group):
        block_key = jax.random.fold_in(key, group)
        hot_key = jax.random.fold_in(hot_base, group % BLOCKS)
        hot = jax.random.randint(hot_key, (), 0, EXPERTS, dtype=jnp.int32)
        raise_key, offset_key, shuffle_key = jax.random.split(block_key, 3)
        raised = jax.random.randint(raise_key, (EXPERTS,), 0, spare + 1, dtype=jnp.int32)
        offset = jax.random.randint(offset_key, (), 1, EXPERTS, dtype=jnp.int32)
        partner = (hot + offset) % EXPERTS
        raised = jnp.where(expert_ids == hot, spare, raised)
        raised = jnp.where(expert_ids == partner, 0, raised)
        counts = per_expert + raised - jnp.take(raised, (expert_ids + offset) % EXPERTS)
        shuffle = jax.random.permutation(shuffle_key, EXPERTS).astype(jnp.int32)
        bounds = jnp.cumsum(jnp.take(counts, shuffle))
        which = jnp.sum((bounds[None, :] <= list_pos[:, None]).astype(jnp.int32), axis=1)
        listed = jnp.take(shuffle, which)
        return listed.reshape(TOPK, BLOCK_TOK).T
    blocks_all = jax.vmap(one_block)(jnp.arange(groups, dtype=jnp.int32))
    return blocks_all.reshape(TOKENS, TOPK).astype(jnp.int32)


def shard_levels(key, extent, pieces, low, top_value):
    factor_of, own = 1.0, jax.random.fold_in(key, 6)
    for axis_at, shards_of in pieces:
        steps = jnp.exp(jax.random.uniform(jax.random.fold_in(own, axis_at), (shards_of,), jnp.float32, low / len(pieces), top_value / len(pieces)))
        factor_of = factor_of * jnp.repeat(steps, extent[axis_at] // shards_of).reshape([-1 if axis == axis_at else 1 for axis in range(len(extent))])
    return factor_of


def scatter_about(own_key, dims, spread, limit, cuts=(), kind=jnp.bfloat16):
    array = jax.random.normal(own_key, dims, jnp.float32) * spread
    if len(cuts) > 0:
        array = shard_levels(own_key, dims, cuts, -0.22, 0.18) * array
    return jnp.clip(array, min=-limit, max=limit).astype(kind)


def setup_inputs(seed: int = 0) -> dict:
    arg_keys = jax.random.split(jax.random.key(seed), 9)
    tokens = draw_tokens(jax.random.fold_in(arg_keys[8], 71), 0)
    norm_gain = jnp.clip(1.0 + 0.15 * jax.random.normal(arg_keys[1], (D,), jnp.float32), 0.25, 1.75).astype(jnp.bfloat16)
    routes = draw_routes(jax.random.fold_in(arg_keys[8], 71), 0)
    route_gates = jnp.clip(jnp.exp(math.log(1.0) - 1.0498221 * jax.random.uniform(arg_keys[3], (TOKENS, TOPK), jnp.float32) ** shard_levels(arg_keys[3], (TOKENS, TOPK), ((0, 128),), -0.2, 0.2)), 0.35, 1.0)
    placement = jax.random.permutation(arg_keys[4], EXPERTS).astype(jnp.int32)
    gate_weight = scatter_about(arg_keys[5], (EXPERTS, D, HID), D ** -0.5, 0.09375, ((0, 128),))
    up_weight = scatter_about(arg_keys[6], (EXPERTS, D, HID), D ** -0.5, 0.09375, ((0, 128),))
    down_weight = scatter_about(arg_keys[7], (EXPERTS, HID, D), HID ** -0.5, 0.21875, ((0, 128),))
    return dict(tokens=tokens, norm_gain=norm_gain, routes=routes, route_gates=route_gates, placement=placement, gate_weight=gate_weight, up_weight=up_weight, down_weight=down_weight)


def reference(tokens, norm_gain, routes, route_gates, placement, gate_weight, up_weight, down_weight):
    values = tokens.astype(jnp.float32)
    rescale = lax.rsqrt(lax.optimization_barrier(jnp.mean(values * values, axis=-1, keepdims=True)) + 1e-06)
    normed = (values * rescale * norm_gain.astype(jnp.float32)).astype(jnp.bfloat16)
    combine_weight = (route_gates / lax.optimization_barrier(jnp.sum(route_gates, axis=-1, keepdims=True))).astype(jnp.bfloat16)
    groups = TOKENS // BLOCK_TOK
    flat_ids = routes.reshape(groups, BLOCK_TOK * TOPK)
    expert_ids = jnp.arange(EXPERTS, dtype=jnp.int32)
    matches = (flat_ids[:, :, None] == expert_ids[None, None, :]).astype(jnp.int32)
    position = lax.optimization_barrier(jnp.sum((jnp.cumsum(matches, axis=1) - matches) * matches, axis=-1)).astype(jnp.int32)
    group_ids = jnp.arange(groups, dtype=jnp.int32)[:, None]
    token_ids = group_ids * BLOCK_TOK + jnp.arange(BLOCK_TOK * TOPK, dtype=jnp.int32)[None, :] // TOPK
    row_slots = (group_ids * CAP + position).astype(jnp.int32)
    source = jnp.full((EXPERTS, groups * CAP), TOKENS, jnp.int32).at[flat_ids, row_slots].set(token_ids)
    shares = jnp.zeros((EXPERTS, groups * CAP), jnp.float32).at[flat_ids, row_slots].set(combine_weight.reshape(groups, BLOCK_TOK * TOPK).astype(jnp.float32))
    padded = jnp.concatenate([normed, jnp.zeros((1, D), jnp.bfloat16)], axis=0)

    def apply_expert(running, stacked):
        gate_mat, up_mat, down_mat, expert = stacked
        row_index = source[expert]
        picked = padded[row_index]
        gate_pre = jnp.dot(picked, gate_mat, preferred_element_type=jnp.float32)
        up_pre = jnp.dot(picked, up_mat, preferred_element_type=jnp.float32)
        hidden = (jax.nn.silu(gate_pre) * up_pre).astype(jnp.bfloat16)
        expert_out = jnp.dot(hidden, down_mat, preferred_element_type=jnp.float32).astype(jnp.bfloat16)
        running = running.at[row_index].add(shares[expert][:, None] * expert_out.astype(jnp.float32))
        return (running, None)
    running, _ = lax.scan(apply_expert, jnp.zeros((TOKENS + 1, D), jnp.float32), (gate_weight, up_weight, down_weight, placement))
    return running[:TOKENS].astype(jnp.bfloat16)
```

```python
import functools

import jax
import jax.numpy as jnp
from jax import lax
from jax.experimental import pallas as pl
from jax.experimental.pallas import tpu as pltpu
from jax.sharding import PartitionSpec as P

MESH = pl.DeviceIdType.MESH
BLOCK_TOK = 32
CAP = 3
EPSILON = 1e-06
SIDE = 4
TOK = 128
TOPK = 8
D = 4096
HID = 768
SLOTS = 12
UNIT = 2 * SLOTS
ROLES = (("x", "y", "z"), ("y", "z", "x"), ("z", "x", "y"))
WIDTH = (1536, 1280, 1280)
START = (0, 1536, 2816)
HALF = tuple(w // 2 for w in WIDTH)
STRIDE = {"x": 16, "y": 4, "z": 1}
STEPS = (0, -1, 1, 2)
VMEM_LIMIT = 62 << 20


def position():
    node, local = lax.axis_index("node"), lax.axis_index("local")
    return {
        "x": (node // 2) % 2 * 2 + local % 2,
        "y": node // 4,
        "z": local // 2,
        "core": node % 2,
    }


def device(at):
    node = (at["y"] * 2 + at["x"] // 2) * 2 + at["core"]
    return node, at["z"] * 2 + at["x"] % 2


def moved(at, axis, by, core=None):
    new = dict(at)
    new[axis] = (at[axis] + by + SIDE) % SIDE
    if core is not None:
        new["core"] = core
    return device(new)


def greet(at):
    barrier = pltpu.get_barrier_semaphore()
    other = 1 - at["core"]
    partners = [moved(at, "x", 0, other)]
    for axis in ("x", "y", "z"):
        for by in (1, -1, 2):
            partners += [moved(at, axis, by), moved(at, axis, by, other)]
    for partner in partners:
        pl.semaphore_signal(barrier, inc=1, device_id=partner, device_id_type=MESH)
    pl.semaphore_wait(barrier, len(partners))


def remote(src, dst, send, recv, target):
    copy = pltpu.make_async_remote_copy(
        src_ref=src, dst_ref=dst, send_sem=send, recv_sem=recv, device_id=target, device_id_type=MESH
    )
    copy.start()


def local_copy(src, dst, sem):
    pltpu.make_async_copy(src, dst, sem).start()


def await_bytes(ref, sem):
    pltpu.make_async_copy(ref, ref, sem).wait()


def tiles(width):
    return [(at, min(256, width - at)) for at in range(0, width, 256)]


def column_codes(meta, group_at, pair):
    codes = []
    for index in range(2):
        for core in range(2):
            lanes = meta[group_at, pair * 2 + index, core]
            codes.append(lanes[:TOPK] * 4.0 + float(index * 2 + core))
    return jnp.concatenate(codes, axis=1)


def dispatch_kernel(
    tokens, gain, own_meta, row_code, gate_w, up_w,
    hidden_out, meta_out0, meta_out1, meta_out2, in0, in1, in2,
    g0, g1, g2, out0, out1, out2, st0, st1, st2, m0, m1, m2, stage, picks, weights, acc,
    w_sem, own_sem, core_send, core_recv, meta_send, meta_recv,
    a_send, a_recv, ah_send, ah_recv, b_send, b_recv, bh_send, bh_recv, row_send, row_recv, stage_sem, end_sem,
):
    at = position()
    core = at["core"]
    other = 1 - core
    gathered, outbox, inbox = (g0, g1, g2), (out0, out1, out2), (in0, in1, in2)
    staged, metas, meta_outs = (st0, st1, st2), (m0, m1, m2), (meta_out0, meta_out1, meta_out2)
    groups = range(3)
    local_copy(gate_w.at[0], weights.at[:, pl.ds(0, HID)], w_sem.at[0])
    local_copy(up_w.at[0], weights.at[:, pl.ds(HID, HID)], w_sem.at[1])

    @pl.loop(0, TOK // 16)
    def _(step):
        rows = pl.ds(pl.multiple_of(step * 16, 16), 16)
        values = tokens[rows, :].astype(jnp.float32)
        rescale = lax.rsqrt(jnp.sum(values * values, axis=-1, keepdims=True) * (1.0 / D) + EPSILON)
        normed = (values * rescale * gain[...].astype(jnp.float32)).astype(jnp.bfloat16)
        for g in groups:
            for h in range(2):
                low = START[g] + h * HALF[g]
                staged[g][h, rows, :] = normed[:, low : low + HALF[g]]

    greet(at)
    for g in groups:
        a, b = at[ROLES[g][0]], at[ROLES[g][1]]
        metas[g][b, a, core] = own_meta[...]
        remote(metas[g].at[b, a, core], metas[g].at[b, a, core], meta_send.at[g, 0], meta_recv.at[g, 0],
               moved(at, "x", 0, other))
        remote(staged[g].at[other], gathered[g].at[b, a, core], core_send.at[g], core_recv.at[g],
               moved(at, "x", 0, other))
        local_copy(staged[g].at[core], gathered[g].at[b, a, core], own_sem.at[g])
    for g in groups:
        axis_a, axis_b, _ = ROLES[g]
        a, b = at[axis_a], at[axis_b]
        await_bytes(metas[g].at[b, a, core], meta_recv.at[g, 0])
        for by in (1, -1, 2):
            remote(metas[g].at[b, a], metas[g].at[b, a], meta_send.at[g, 1], meta_recv.at[g, 1], moved(at, axis_a, by))
        await_bytes(gathered[g].at[b, a, core], own_sem.at[g])
        await_bytes(gathered[g].at[b, a, core], core_recv.at[g])
        for way, by in enumerate((1, -1)):
            remote(gathered[g].at[b, a], gathered[g].at[b, a], a_send.at[g, way], a_recv.at[g, way], moved(at, axis_a, by))

    def spread_b(g, order, a_from):
        axis_b = ROLES[g][1]
        b = at[axis_b]
        for way, by in enumerate((1, -1)):
            remote(gathered[g].at[b, a_from], gathered[g].at[b, a_from], b_send.at[g, order, way], b_recv.at[g, order, way],
                   moved(at, axis_b, by))

    for g in groups:
        spread_b(g, 0, at[ROLES[g][0]])
    for g in groups:
        axis_a, axis_b, _ = ROLES[g]
        a, b = at[axis_a], at[axis_b]
        await_bytes(metas[g].at[0, pl.ds(0, 3)], meta_recv.at[g, 1])
        for by in (1, -1, 2):
            remote(metas[g].at[b], metas[g].at[b], meta_send.at[g, 2], meta_recv.at[g, 2], moved(at, axis_b, by))
    for way, by in enumerate((1, -1)):
        for g in groups:
            axis_a, axis_b, _ = ROLES[g]
            b = at[axis_b]
            a_from = (at[axis_a] - by + SIDE) % SIDE
            await_bytes(gathered[g].at[b, a_from], a_recv.at[g, way])
            remote(gathered[g].at[b, a_from, way], gathered[g].at[b, a_from, way], ah_send.at[g, way], ah_recv.at[g, way],
                   moved(at, axis_a, by))
            spread_b(g, 1 + way, a_from)
    for g in groups:
        axis_a, axis_b, _ = ROLES[g]
        b = at[axis_b]
        a_from = (at[axis_a] + 2) % SIDE
        for way in range(2):
            await_bytes(gathered[g].at[b, a_from, way], ah_recv.at[g, way])
        spread_b(g, 3, a_from)

    @pl.loop(0, 64)
    def _(unit):
        acc[unit] = jnp.zeros((UNIT, 2 * HID), jnp.float32)

    for g in groups:
        await_bytes(metas[g].at[pl.ds(0, 3)], meta_recv.at[g, 2])

    def pick_and_send(g, order):
        _, axis_b, axis_c = ROLES[g]
        b_from = (at[axis_b] + STEPS[order] + SIDE) % SIDE

        @pl.loop(0, 2)
        def _(pair):
            codes = column_codes(metas[g], b_from, pair)
            rows = row_code[g]
            found = rows == codes[0:1]
            for k in range(1, TOPK):
                found = jnp.logical_or(found, rows == codes[k : k + 1])
            picks[...] = jnp.where(found, 1.0, 0.0).astype(jnp.bfloat16)
            for low, size in tiles(HALF[g]):
                block = gathered[g][b_from, pl.ds(pair * 2, 2), :, :, low : low + size].reshape(512, size)
                picked = jnp.dot(picks[...], block, preferred_element_type=jnp.float32)
                outbox[g][order, :, pair, :, low : low + size] = picked.astype(jnp.bfloat16).reshape(8, 48, size)

        c = at[axis_c]
        for by in (1, -1, 2, 0):
            c_to = (c + by + SIDE) % SIDE
            for k in range(2):
                core_to = (core + k) % 2
                box = outbox[g].at[order, c_to * 2 + core_to]
                slot = inbox[g].at[order, core, c]
                if by == 0 and k == 0:
                    local_copy(box, slot, row_recv.at[g, order])
                else:
                    remote(box, slot, row_send.at[g, order], row_recv.at[g, order], moved(at, axis_c, by, core_to))

    def multiply(g, order):
        axis_a, axis_b, axis_c = ROLES[g]
        b_from = (at[axis_b] + STEPS[order] + SIDE) % SIDE
        await_bytes(inbox[g].at[order], row_recv.at[g, order])
        view = stage.at[:, :, :, :, pl.ds(0, HALF[g])]
        copy = pltpu.make_async_copy(inbox[g].at[order], view, stage_sem.at[0])
        copy.start()
        copy.wait()

        @pl.loop(0, 2 * HID // 256)
        def _(tile):
            columns = pl.ds(pl.multiple_of(tile * 256, 256), 256)
            total = None
            for h in range(2):
                rows = stage[h, :, :, :, 0 : HALF[g]].reshape(384, HALF[g])
                part = jnp.dot(rows, weights[START[g] + h * HALF[g] : START[g] + (h + 1) * HALF[g], columns],
                               preferred_element_type=jnp.float32)
                total = part if total is None else total + part
            for c in range(SIDE):
                for a in range(SIDE):
                    unit = a * STRIDE[axis_a] + b_from * STRIDE[axis_b] + c * STRIDE[axis_c]
                    low = (c * SIDE + a) * UNIT
                    acc[unit, :, columns] += total[low : low + UNIT]

    for g in groups:
        pick_and_send(g, 0)
    for order in range(4):
        for way, by in enumerate((1, -1)):
            for g in groups:
                axis_a, axis_b, _ = ROLES[g]
                a_from = (at[axis_a] + (0, -1, 1, 2)[order] + SIDE) % SIDE
                b_from = (at[axis_b] - by + SIDE) % SIDE
                await_bytes(gathered[g].at[b_from, a_from], b_recv.at[g, order, way])
                remote(gathered[g].at[b_from, a_from, way], gathered[g].at[b_from, a_from, way],
                       bh_send.at[g, order, way], bh_recv.at[g, order, way], moved(at, axis_b, by))
    await_bytes(weights.at[:, pl.ds(0, HID)], w_sem.at[0])
    await_bytes(weights.at[:, pl.ds(HID, HID)], w_sem.at[1])
    for g in groups:
        pick_and_send(g, 1)
        pick_and_send(g, 2)
    for g in groups:
        multiply(g, 0)
    for g in groups:
        axis_a, axis_b, _ = ROLES[g]
        for order in range(4):
            a_from = (at[axis_a] + (0, -1, 1, 2)[order] + SIDE) % SIDE
            for way in range(2):
                b_from = (at[axis_b] + 2) % SIDE
                await_bytes(gathered[g].at[b_from, a_from, way], bh_recv.at[g, order, way])
        pick_and_send(g, 3)
    for order in (1, 2, 3):
        for g in groups:
            multiply(g, order)

    @pl.loop(0, 64)
    def _(unit):
        gate, up = acc[unit, :, 0:HID], acc[unit, :, HID : 2 * HID]
        hidden = gate / (1.0 + jnp.exp(-gate)) * up
        acc[unit, :, 0:HID] = hidden.astype(jnp.bfloat16).astype(jnp.float32)

    ending = [pltpu.make_async_copy(acc.at[:, :, pl.ds(0, HID)], hidden_out, end_sem.at[3])]
    ending += [pltpu.make_async_copy(metas[g], meta_outs[g], end_sem.at[g]) for g in groups]
    for copy in ending:
        copy.start()
    for g in groups:
        a, b = at[ROLES[g][0]], at[ROLES[g][1]]
        await_bytes(metas[g].at[b, a, core], meta_send.at[g, 0])
        await_bytes(metas[g].at[0, pl.ds(0, 3)], meta_send.at[g, 1])
        await_bytes(metas[g].at[pl.ds(0, 3)], meta_send.at[g, 2])
        await_bytes(staged[g].at[other], core_send.at[g])
        for way in range(2):
            await_bytes(gathered[g].at[b, a], a_send.at[g, way])
            await_bytes(gathered[g].at[b, a, 0], ah_send.at[g, way])
            for order in range(4):
                await_bytes(gathered[g].at[b, a], b_send.at[g, order, way])
                await_bytes(gathered[g].at[b, a, 0], bh_send.at[g, order, way])
        for order in range(4):
            await_bytes(outbox[g].at[order, pl.ds(0, 7)], row_send.at[g, order])
    for copy in ending:
        copy.wait()


def return_kernel(
    hidden, meta0, meta1, meta2, row_code, down_w,
    result, in0, in1, in2, l0, l1, l2,
    weights, out0, out1, out2, p0, p1, p2, own, stage, low_a, low_b, s0, s1, s2, r0, r1, r2, f0, f1, f2, last, end0, end1, end2,
    share, rows_bf,
    w_sem, row_send, row_recv, b_send, b_recv, a_send, a_recv, core_send, core_recv, stage_sem, end_sem,
):
    at = position()
    core = at["core"]
    other = 1 - core
    groups = range(3)
    metas, inbox, outbox = (meta0, meta1, meta2), (in0, in1, in2), (out0, out1, out2)
    partial, landed = (p0, p1, p2), (l0, l1, l2)
    sums, arrived, final, ends = (s0, s1, s2), (r0, r1, r2), (f0, f1, f2), (end0, end1, end2)
    weight_copy = pltpu.make_async_copy(down_w.at[0], weights, w_sem.at[0])
    weight_copy.start()
    greet(at)
    weight_copy.wait()

    def expand_and_send(g, order):
        axis_a, axis_b, axis_c = ROLES[g]
        b_to = (at[axis_b] + STEPS[order] + SIDE) % SIDE
        for c in range(SIDE):
            units = [
                hidden[a * STRIDE[axis_a] + b_to * STRIDE[axis_b] + c * STRIDE[axis_c]] for a in range(SIDE)
            ]
            rows_bf[c * 96 : (c + 1) * 96, :] = jnp.concatenate(units, axis=0).astype(jnp.bfloat16)
        for h in range(2):
            for low, size in tiles(HALF[g]):
                first = START[g] + h * HALF[g] + low
                made = jnp.dot(rows_bf[...], weights[:, first : first + size], preferred_element_type=jnp.float32)
                outbox[g][order, h, :, :, :, low : low + size] = made.astype(jnp.bfloat16).reshape(4, 2, 48, size)
        c = at[axis_c]
        for by in (1, -1, 2, 0):
            c_to = (c + by + SIDE) % SIDE
            for k in range(2):
                core_to = (core + k) % 2
                box = outbox[g].at[order, core_to, c_to]
                slot = inbox[g].at[order, c * 2 + core]
                if by == 0 and k == 0:
                    local_copy(box, slot, row_recv.at[g, order])
                else:
                    remote(box, slot, row_send.at[g, order], row_recv.at[g, order], moved(at, axis_c, by, core_to))

    def combine(g, order, place):
        _, axis_b, _ = ROLES[g]
        b_to = (at[axis_b] + STEPS[order] + SIDE) % SIDE
        await_bytes(inbox[g].at[order], row_recv.at[g, order])
        view = stage.at[:, :, :, pl.ds(0, HALF[g])]
        copy = pltpu.make_async_copy(inbox[g].at[order], view, stage_sem.at[0])
        copy.start()
        copy.wait()

        @pl.loop(0, 2)
        def _(pair):
            codes = column_codes(metas[g], b_to, pair)
            scale = jnp.concatenate(
                [metas[g][b_to, pair * 2 + i, k][TOPK:] for i in range(2) for k in range(2)], axis=1
            )
            rows = row_code[g]
            total = jnp.where(rows == codes[0:1], scale[0:1], 0.0)
            for k in range(1, TOPK):
                total = jnp.where(rows == codes[k : k + 1], scale[k : k + 1], total)
            share[...] = total.T.astype(jnp.bfloat16)
            for low, size in tiles(HALF[g]):
                block = stage[:, pair, :, low : low + size].reshape(384, size)
                mixed = jnp.dot(share[...], block, preferred_element_type=jnp.float32)
                place(pair, low, size, mixed.reshape(2, 2, TOK, size))

    def load(source, target):
        copy = pltpu.make_async_copy(source, target, stage_sem.at[1])
        copy.start()
        copy.wait()

    def far(g):
        def place(pair, low, size, block):
            for i in range(2):
                for half in range(2):
                    partial[g][0, half, pair * 2 + i, :, low : low + size] = block[i, half].astype(jnp.bfloat16)

        combine(g, 3, place)
        for half, by in enumerate((1, -1)):
            remote(partial[g].at[0, half], landed[g].at[half, 0], b_send.at[g, half], b_recv.at[g, half],
                   moved(at, ROLES[g][1], by))

    def near(g, order):
        by = STEPS[order]
        half_in = 0 if by == 1 else 1
        await_bytes(landed[g].at[half_in, 0], b_recv.at[g, half_in])
        load(landed[g].at[half_in, 0], low_a.at[0, :, :, pl.ds(0, HALF[g])])

        def place(pair, low, size, block):
            for i in range(2):
                for half in range(2):
                    value = block[i, half]
                    if half == half_in:
                        value = value + low_a[0, pair * 2 + i, :, low : low + size].astype(jnp.float32)
                    partial[g][order, half, pair * 2 + i, :, low : low + size] = value.astype(jnp.bfloat16)

        combine(g, order, place)
        index = 2 + half_in
        remote(partial[g].at[order], landed[g].at[pl.ds(2 + 2 * half_in, 2), 0], b_send.at[g, index], b_recv.at[g, index],
               moved(at, ROLES[g][1], by))

    def home(g):
        axis_a = ROLES[g][0]
        a = at[axis_a]
        wide = pl.ds(0, HALF[g])

        def place(pair, low, size, block):
            for i in range(2):
                for half in range(2):
                    own[pair * 2 + i, half, :, low : low + size] = block[i, half]

        combine(g, 0, place)
        for index in range(2):
            await_bytes(landed[g].at[pl.ds(2 + 2 * index, 2), 0], b_recv.at[g, 2 + index])
        load(landed[g].at[pl.ds(2, 2), 0], low_a.at[:, :, :, wide])
        load(landed[g].at[pl.ds(4, 2), 0], low_b.at[:, :, :, wide])

        def settled(a_to, half):
            value = own[a_to, half, :, 0 : HALF[g]]
            value = value + low_a[half, a_to, :, 0 : HALF[g]].astype(jnp.float32)
            return value + low_b[half, a_to, :, 0 : HALF[g]].astype(jnp.float32)

        opposite = (a + 2) % SIDE
        for half, by in enumerate((1, -1)):
            sums[g][0, half] = settled(opposite, half).astype(jnp.bfloat16)
            remote(sums[g].at[0, half], arrived[g].at[half], a_send.at[g, half], a_recv.at[g, half], moved(at, axis_a, by))
        for half_in, by in enumerate((1, -1)):
            a_to = (a + by + SIDE) % SIDE
            await_bytes(arrived[g].at[half_in], a_recv.at[g, half_in])
            for half in range(2):
                value = settled(a_to, half)
                if half == half_in:
                    value = value + arrived[g][half_in].astype(jnp.float32)
                sums[g][1 + half_in, half] = value.astype(jnp.bfloat16)
            index = 2 + half_in
            remote(sums[g].at[1 + half_in], arrived[g].at[pl.ds(2 + 2 * half_in, 2)], a_send.at[g, index],
                   a_recv.at[g, index], moved(at, axis_a, by))
        for half in range(2):
            final[g][half] = settled(a, half)

    def finish(g):
        for index in range(2):
            await_bytes(arrived[g].at[pl.ds(2 + 2 * index, 2)], a_recv.at[g, 2 + index])
        for half in range(2):
            value = final[g][half] + arrived[g][2 + half].astype(jnp.float32) + arrived[g][4 + half].astype(jnp.float32)
            last[half, :, START[g] // 2 : START[g] // 2 + HALF[g]] = value.astype(jnp.bfloat16)
        span = pl.ds(START[g] // 2, HALF[g])
        remote(last.at[other, :, span], ends[g], core_send.at[g], core_recv.at[g], moved(at, "x", 0, other))

    for order in (3, 1, 2, 0):
        for g in groups:
            expand_and_send(g, order)
    for g in groups:
        far(g)
    for g in groups:
        near(g, 1)
        near(g, 2)
    for g in groups:
        home(g)
    for g in groups:
        finish(g)
    for g in groups:
        mine = last[core, :, START[g] // 2 : START[g] // 2 + HALF[g]]
        await_bytes(ends[g], core_recv.at[g])
        theirs = ends[g][...]
        first, second = jnp.where(core == 0, mine, theirs), jnp.where(core == 0, theirs, mine)
        result[:, START[g] : START[g] + HALF[g]] = first
        result[:, START[g] + HALF[g] : START[g] + WIDTH[g]] = second
    for g in groups:
        for order in range(4):
            await_bytes(inbox[g].at[order, pl.ds(0, 7)], row_send.at[g, order])
        for half in range(2):
            await_bytes(partial[g].at[0, half], b_send.at[g, half])
            await_bytes(partial[g].at[0], b_send.at[g, 2 + half])
            await_bytes(sums[g].at[0, half], a_send.at[g, half])
            await_bytes(sums[g].at[0], a_send.at[g, 2 + half])
        await_bytes(ends[g], core_send.at[g])


def body(tokens, norm_gain, routes, route_gates, placement, gate_weight, up_weight, down_weight):
    experts = placement.shape[0]
    blocks = TOK // BLOCK_TOK
    bf16, f32 = jnp.bfloat16, jnp.float32
    combine_weight = (route_gates / jnp.sum(route_gates, axis=-1, keepdims=True)).astype(bf16)
    expert_ids = jnp.arange(experts, dtype=jnp.int32)
    holder = jnp.sum(jnp.where(placement[None, :] == expert_ids[:, None], expert_ids[None, :], 0), axis=1)
    one_hot = routes[:, :, None] == expert_ids
    target = jnp.sum(jnp.where(one_hot, holder, 0), axis=-1)
    named = jnp.any(one_hot, axis=1).astype(f32).reshape(blocks, BLOCK_TOK, experts)
    before = jnp.einsum("ts,bse->bte", jnp.tril(jnp.ones((BLOCK_TOK, BLOCK_TOK), f32), -1), named)
    position_in = jnp.sum(jnp.where(one_hot, before.reshape(TOK, 1, experts), 0.0), axis=-1)
    block = (jnp.arange(TOK) // BLOCK_TOK).astype(f32)[:, None]
    code = target.astype(f32) * SLOTS + block * CAP + position_in
    own_meta = jnp.concatenate([code.T, combine_weight.astype(f32).T], axis=0)

    at = position()
    row = jnp.arange(384)
    line, core_to, inner = row // 96, row // 48 % 2, row % 48
    tables = []
    for roles in ROLES:
        spot = dict(at)
        spot[roles[2]] = line
        spot["core"] = core_to
        node, local = device(spot)
        tables.append(((node * 8 + local) * SLOTS + inner % SLOTS) * 4 + inner // SLOTS)
    row_code = jnp.stack(tables).astype(f32)[:, :, None]

    vmem, hbm = pl.BlockSpec(memory_space=pltpu.VMEM), pl.BlockSpec(memory_space=pltpu.HBM)
    dma = pltpu.SemaphoreType.DMA
    shape = jax.ShapeDtypeStruct
    meta_shape = (SIDE, SIDE, 2, 2 * TOPK, TOK)
    boxes = [(4, 2, 4, 2, 48, h) for h in HALF]
    hidden, meta0, meta1, meta2, *_ = pl.pallas_call(
        dispatch_kernel,
        out_shape=[shape((64, UNIT, HID), f32)] + [shape(meta_shape, f32)] * 3 + [shape(b, bf16) for b in boxes],
        in_specs=[vmem] * 4 + [hbm] * 2,
        out_specs=[hbm] * 7,
        scratch_shapes=[pltpu.VMEM((SIDE, SIDE, 2, TOK, h), bf16) for h in HALF]
        + [pltpu.VMEM((4, 8, 2, 48, h), bf16) for h in HALF]
        + [pltpu.VMEM((2, TOK, h), bf16) for h in HALF]
        + [pltpu.VMEM(meta_shape, f32)] * 3
        + [
            pltpu.VMEM((2, 4, 2, 48, max(HALF)), bf16),
            pltpu.VMEM((384, 512), bf16),
            pltpu.VMEM((D, 2 * HID), bf16),
            pltpu.VMEM((64, UNIT, 2 * HID), f32),
            dma((2,)), dma((3,)), dma((3,)), dma((3,)), dma((3, 3)), dma((3, 3)),
            dma((3, 2)), dma((3, 2)), dma((3, 2)), dma((3, 2)),
            dma((3, 4, 2)), dma((3, 4, 2)), dma((3, 4, 2)), dma((3, 4, 2)),
            dma((3, 4)), dma((3, 4)), dma((1,)), dma((4,)),
        ],
        compiler_params=pltpu.CompilerParams(collective_id=0, has_side_effects=True, vmem_limit_bytes=VMEM_LIMIT),
        name="dispatch",
    )(tokens, norm_gain[None, :], own_meta, row_code, gate_weight, up_weight)

    result, *_ = pl.pallas_call(
        return_kernel,
        out_shape=[shape((TOK, D), bf16)]
        + [shape((4, 8, 2, 48, h), bf16) for h in HALF]
        + [shape((6, 1, SIDE, TOK, h), bf16) for h in HALF],
        in_specs=[vmem] * 5 + [hbm],
        out_specs=[vmem] + [hbm] * 6,
        scratch_shapes=[pltpu.VMEM((HID, D), bf16)]
        + [pltpu.VMEM(b, bf16) for b in boxes]
        + [pltpu.VMEM((3, 2, SIDE, TOK, h), bf16) for h in HALF]
        + [
            pltpu.VMEM((SIDE, 2, TOK, max(HALF)), f32),
            pltpu.VMEM((8, 2, 48, max(HALF)), bf16),
            pltpu.VMEM((2, SIDE, TOK, max(HALF)), bf16),
            pltpu.VMEM((2, SIDE, TOK, max(HALF)), bf16),
        ]
        + [pltpu.VMEM((3, 2, TOK, h), bf16) for h in HALF]
        + [pltpu.VMEM((6, TOK, h), bf16) for h in HALF]
        + [pltpu.VMEM((2, TOK, h), f32) for h in HALF]
        + [pltpu.VMEM((2, TOK, D // 2), bf16)]
        + [pltpu.VMEM((TOK, h), bf16) for h in HALF]
        + [
            pltpu.VMEM((512, 384), bf16),
            pltpu.VMEM((384, HID), bf16),
            dma((1,)), dma((3, 4)), dma((3, 4)), dma((3, 4)), dma((3, 4)), dma((3, 4)), dma((3, 4)),
            dma((3,)), dma((3,)), dma((2,)), dma((1,)),
        ],
        compiler_params=pltpu.CompilerParams(collective_id=1, has_side_effects=True, vmem_limit_bytes=VMEM_LIMIT),
        name="give_back",
    )(hidden, meta0, meta1, meta2, row_code, down_weight)
    return result


def solution(mesh):
    rows = P(("node", "local"), None)
    whole = P(("node", "local"), None, None)
    in_specs = (rows, P(), rows, rows, P(), whole, whole, whole)
    return jax.shard_map(body, mesh=mesh, in_specs=in_specs, out_specs=rows, check_vma=False)
```

```python
import jax
import jax.numpy as jnp
import numpy as np
from jax import lax
from jax.experimental import pallas as pl
from jax.experimental.pallas import tpu as pltpu
from jax.sharding import PartitionSpec as P

MESH = pl.DeviceIdType.MESH
BLOCK_TOK = 32
CAP = 3
EPSILON = 1e-06
SIDE = 4
TOK = 128
TOPK = 8
D = 4096
HID = 768
SLOTS = 12
UNIT = 2 * SLOTS
ROLES = (("x", "y", "z"), ("y", "z", "x"), ("z", "x", "y"))
WIDTH = (1536, 1280, 1280)
START = (0, 1536, 2816)
HALF = tuple(w // 2 for w in WIDTH)
WIDE = max(HALF)
STRIDE = {"x": 16, "y": 4, "z": 1}
STEPS = (0, -1, 1, 2)
RETURNS = {
    (0, 0): (0, 0), (0, 1): (0, 0),
    (1, 0): (2, 0), (1, 1): (1, -1),
    (2, 0): (1, 1), (2, 1): (2, 0),
    (3, 0): (3, -1), (3, 1): (3, 1),
}
VMEM_LIMIT = 62 << 20


def position():
    node, local = lax.axis_index("node"), lax.axis_index("local")
    return {
        "x": (node // 2) % 2 * 2 + local % 2,
        "y": node // 4,
        "z": local // 2,
        "core": node % 2,
    }


def device(at):
    node = (at["y"] * 2 + at["x"] // 2) * 2 + at["core"]
    return node, at["z"] * 2 + at["x"] % 2


def step_on(value, by):
    return (value + by + SIDE) % SIDE


def moved(at, axis, by, core=None, axis2=None, by2=0):
    new = dict(at)
    new[axis] = step_on(at[axis], by)
    if axis2 is not None:
        new[axis2] = step_on(at[axis2], by2)
    if core is not None:
        new["core"] = core
    return device(new)


def greet(at):
    barrier = pltpu.get_barrier_semaphore()
    other = 1 - at["core"]
    partners = [moved(at, "x", 0, other)]
    for _, axis_b, axis_c in ROLES:
        for by in (1, -1, 2):
            for core in (at["core"], other):
                partners.append(moved(at, axis_c, by, core))
                for side in (1, -1):
                    partners.append(moved(at, axis_c, by, core, axis_b, side))
    for partner in partners:
        pl.semaphore_signal(barrier, inc=1, device_id=partner, device_id_type=MESH)
    pl.semaphore_wait(barrier, len(partners))


def remote(src, dst, send, recv, target):
    pltpu.make_async_remote_copy(
        src_ref=src, dst_ref=dst, send_sem=send, recv_sem=recv, device_id=target, device_id_type=MESH
    ).start()


def local_copy(src, dst, sem):
    pltpu.make_async_copy(src, dst, sem).start()


def await_bytes(ref, sem):
    pltpu.make_async_copy(ref, ref, sem).wait()


def tiles(width):
    return [(at, min(256, width - at)) for at in range(0, width, 256)]


def kernel(
    tokens, gain, own_meta, pattern, gate_w, up_w, down_w,
    result, in0, in1, in2, back0, back1, back2, land0, land1, land2,
    g0, g1, g2, n0, n1, n2, out0, out1, out2, st0, st1, st2, m0, m1, m2, k0, k1, k2,
    stage, share, rows_bf, weights, acc, own2, low, r0, r1, r2, last, end0, end1, end2,
    w_sem, own_sem, core_send, core_recv, meta_send, meta_recv, a_send, a_recv, ah_send, ah_recv, b_send, b_recv,
    row_send, row_recv, stage_sem, back_send, back_recv, sum_send, sum_recv, c_send, c_recv, end_send, end_recv,
):
    at = position()
    core = at["core"]
    other = 1 - core
    groups = range(3)
    gathered, near, outbox, inbox = (g0, g1, g2), (n0, n1, n2), (out0, out1, out2), (in0, in1, in2)
    staged, metas, near_metas = (st0, st1, st2), (m0, m1, m2), (k0, k1, k2)
    backbox, landed, arrived, ends = (back0, back1, back2), (land0, land1, land2), (r0, r1, r2), (end0, end1, end2)
    local_copy(gate_w.at[0], weights.at[:, pl.ds(0, HID)], w_sem.at[0])
    local_copy(up_w.at[0], weights.at[:, pl.ds(HID, HID)], w_sem.at[1])

    @pl.loop(0, TOK // 16)
    def _(step):
        rows = pl.ds(pl.multiple_of(step * 16, 16), 16)
        values = tokens[rows, :].astype(jnp.float32)
        rescale = lax.rsqrt(jnp.sum(values * values, axis=-1, keepdims=True) * (1.0 / D) + EPSILON)
        normed = (values * rescale * gain[...].astype(jnp.float32)).astype(jnp.bfloat16)
        for g in groups:
            for h in range(2):
                low_at = START[g] + h * HALF[g]
                staged[g][h, rows, :] = normed[:, low_at : low_at + HALF[g]]

    greet(at)
    for g in groups:
        a = at[ROLES[g][0]]
        metas[g][a, core] = own_meta[...]
        remote(metas[g].at[a, core], metas[g].at[a, core], meta_send.at[g, 0], meta_recv.at[g, 0], moved(at, "x", 0, other))
        remote(staged[g].at[other], gathered[g].at[a, core], core_send.at[g], core_recv.at[g], moved(at, "x", 0, other))
        local_copy(staged[g].at[core], gathered[g].at[a, core], own_sem.at[g])

    def spread(g, order, a_from):
        pair = a_from // 2
        remote(gathered[g].at[a_from], near[g].at[pair, a_from % 2], b_send.at[g, order], b_recv.at[g, pair],
               moved(at, ROLES[g][1], 1 - 2 * pair))

    for g in groups:
        axis_a = ROLES[g][0]
        a = at[axis_a]
        await_bytes(gathered[g].at[a, core], own_sem.at[g])
        await_bytes(gathered[g].at[a, core], core_recv.at[g])
        for way, by in enumerate((1, -1)):
            remote(gathered[g].at[a], gathered[g].at[a], a_send.at[g, way], a_recv.at[g, way], moved(at, axis_a, by))
        await_bytes(metas[g].at[a, core], meta_recv.at[g, 0])
        for by in (1, -1, 2):
            remote(metas[g].at[a], metas[g].at[a], meta_send.at[g, 1], meta_recv.at[g, 1], moved(at, axis_a, by))
    for g in groups:
        spread(g, 0, at[ROLES[g][0]])
    for g in groups:
        await_bytes(metas[g].at[pl.ds(0, 3)], meta_recv.at[g, 1])
        for pair in range(2):
            remote(metas[g].at[pl.ds(2 * pair, 2)], near_metas[g].at[pair], meta_send.at[g, 2], meta_recv.at[g, 2],
                   moved(at, ROLES[g][1], 1 - 2 * pair))

    @pl.loop(0, 64)
    def _(unit):
        acc[pl.ds(pl.multiple_of(unit * UNIT, 8), UNIT), :] = jnp.zeros((UNIT, 2 * HID), jnp.float32)

    for way, by in enumerate((1, -1)):
        for g in groups:
            axis_a = ROLES[g][0]
            a_from = step_on(at[axis_a], -by)
            await_bytes(gathered[g].at[a_from], a_recv.at[g, way])
            remote(gathered[g].at[a_from, way], gathered[g].at[a_from, way], ah_send.at[g, way], ah_recv.at[g, way],
                   moved(at, axis_a, by))
            spread(g, 1 + way, a_from)
    for g in groups:
        a_from = step_on(at[ROLES[g][0]], 2)
        for way in range(2):
            await_bytes(gathered[g].at[a_from, way], ah_recv.at[g, way])
        spread(g, 3, a_from)

    def line_base(g, by):
        _, axis_b, axis_c = ROLES[g]
        spot = dict(at)
        spot[axis_b] = step_on(at[axis_b], by)
        spot[axis_c] = 0
        spot["core"] = 0
        node, local = device(spot)
        return ((node * 8 + local) * (4 * SLOTS)).astype(jnp.float32)

    def meta_of(g, is_near, pair, index, k):
        return near_metas[g][pair, index, k] if is_near else metas[g][pair * 2 + index, k]

    def column_codes(g, is_near, pair):
        return jnp.concatenate(
            [meta_of(g, is_near, pair, i, k)[:TOPK] * 4.0 + float(i * 2 + k) for i in range(2) for k in range(2)], axis=1
        )

    def pick_and_send(g, kind):
        _, axis_b, axis_c = ROLES[g]
        is_near = kind >= 2

        @pl.loop(0, 2)
        def _(pair):
            if kind == 3:
                await_bytes(near[g].at[pair], b_recv.at[g, pair])
            ahead = 1 - 2 * pair
            by_b = (0, -ahead, 0, ahead)[kind]
            order = (0, 2 - pair, 1 + pair, 3)[kind]
            codes = column_codes(g, is_near, pair)
            rows = pattern[g] + line_base(g, by_b)
            found = rows == codes[0:1]
            for k in range(1, TOPK):
                found = jnp.logical_or(found, rows == codes[k : k + 1])
            share[0:384, 0:512] = jnp.where(found, 1.0, 0.0).astype(jnp.bfloat16)
            for low_at, size in tiles(HALF[g]):
                span = slice(low_at, low_at + size)
                if is_near:
                    block = near[g][pair, :, :, :, span]
                else:
                    block = gathered[g][pl.ds(pair * 2, 2), :, :, span]
                picked = jnp.dot(share[0:384, 0:512], block.reshape(512, size), preferred_element_type=jnp.float32)
                outbox[g][kind * 2 + pair, :, :, span] = picked.astype(jnp.bfloat16).reshape(8, 48, size)
            c = at[axis_c]
            for by in (1, -1, 2, 0):
                c_to = step_on(c, by)
                for k in range(2):
                    core_to = (core + k) % 2
                    box = outbox[g].at[kind * 2 + pair, c_to * 2 + core_to]
                    slot = inbox[g].at[order, core, c, pair]
                    if by == 0 and k == 0 and kind in (0, 2):
                        local_copy(box, slot, row_recv.at[g, order])
                    else:
                        remote(box, slot, row_send.at[g, kind], row_recv.at[g, order],
                               moved(at, axis_c, by, core_to, axis_b, by_b))

    def multiply(g, order):
        axis_a, axis_b, axis_c = ROLES[g]
        b_from = step_on(at[axis_b], STEPS[order])
        await_bytes(inbox[g].at[order], row_recv.at[g, order])
        copy = pltpu.make_async_copy(inbox[g].at[order], stage.at[:, :, :, :, pl.ds(0, HALF[g])], stage_sem.at[0])
        copy.start()
        copy.wait()

        @pl.loop(0, 2 * HID // 256)
        def _(tile):
            columns = pl.ds(pl.multiple_of(tile * 256, 256), 256)
            total = None
            for h in range(2):
                rows = stage[h, :, :, :, 0 : HALF[g]].reshape(384, HALF[g])
                part = jnp.dot(rows, weights[START[g] + h * HALF[g] : START[g] + (h + 1) * HALF[g], columns],
                               preferred_element_type=jnp.float32)
                total = part if total is None else total + part
            for c in range(SIDE):
                for a in range(SIDE):
                    unit = a * STRIDE[axis_a] + b_from * STRIDE[axis_b] + c * STRIDE[axis_c]
                    low_at = (c * SIDE + a) * UNIT
                    acc[pl.ds(pl.multiple_of(unit * UNIT, 8), UNIT), columns] += total[low_at : low_at + UNIT]

    for kind in (0, 1):
        for g in groups:
            pick_and_send(g, kind)
    for g in groups:
        await_bytes(near_metas[g], meta_recv.at[g, 2])
    for kind in (3, 2):
        for g in groups:
            pick_and_send(g, kind)
    await_bytes(weights.at[:, pl.ds(0, HID)], w_sem.at[0])
    await_bytes(weights.at[:, pl.ds(HID, HID)], w_sem.at[1])

    def down_of(g):
        return weights.at[pl.ds(g * HID, HID), pl.ds(0, WIDTH[g])]

    def fetch_down(g):
        local_copy(down_w.at[0, :, pl.ds(START[g], WIDTH[g])], down_of(g), w_sem.at[2 + g])

    for order in (0, 3, 1, 2):
        for g in groups:
            multiply(g, order)
            if order == 2 and g == 0:
                fetch_down(0)
                fetch_down(1)
            if order == 2 and g == 1:
                fetch_down(2)

    @pl.loop(0, 64)
    def _(unit):
        rows = pl.ds(pl.multiple_of(unit * UNIT, 8), UNIT)
        gate, up = acc[rows, 0:HID], acc[rows, HID : 2 * HID]
        hidden = gate / (1.0 + jnp.exp(-gate)) * up
        acc[rows, 0:HID] = hidden.astype(jnp.bfloat16).astype(jnp.float32)

    for g in groups:
        for kind in range(4):
            count = 7 if kind in (0, 2) else 8
            await_bytes(outbox[g].at[pl.ds(0, 2), pl.ds(0, count)], row_send.at[g, kind])
    for g in groups:
        await_bytes(down_of(g), w_sem.at[2 + g])

    def expand_and_send(g, order):
        axis_a, axis_b, axis_c = ROLES[g]
        b_to = step_on(at[axis_b], STEPS[order])
        for c in range(SIDE):
            units = [
                acc[pl.ds(pl.multiple_of(
                    (a * STRIDE[axis_a] + b_to * STRIDE[axis_b] + c * STRIDE[axis_c]) * UNIT, 8), UNIT), 0:HID]
                for a in range(SIDE)
            ]
            rows_bf[c * 96 : (c + 1) * 96, :] = jnp.concatenate(units, axis=0).astype(jnp.bfloat16)

        @pl.loop(0, 2)
        def _(h):
            for low_at, size in tiles(HALF[g]):
                columns = pl.ds(pl.multiple_of(h * HALF[g] + low_at, 128), size)
                made = jnp.dot(rows_bf[...], weights[g * HID : (g + 1) * HID, columns], preferred_element_type=jnp.float32)
                made = made.astype(jnp.bfloat16).reshape(SIDE, 2, 48, size)
                for pair in range(2):
                    outbox[g][order * 2 + pair, pl.ds(h * SIDE, SIDE), :, low_at : low_at + size] = made[:, pair]

        c = at[axis_c]
        for pair in range(2):
            kind, by_b = RETURNS[order, pair]
            for by in (1, -1, 2, 0):
                c_to = step_on(c, by)
                for k in range(2):
                    core_to = (core + k) % 2
                    box = outbox[g].at[order * 2 + pair, core_to * SIDE + c_to]
                    slot = backbox[g].at[kind // 2, pair, kind % 2, c * 2 + core]
                    sem = back_recv.at[g, kind // 2, pair]
                    if by == 0 and k == 0 and by_b == 0:
                        local_copy(box, slot, sem)
                    else:
                        remote(box, slot, back_send.at[g, order, pair], sem, moved(at, axis_c, by, core_to, axis_b, by_b))

    def load(source, target, sem):
        copy = pltpu.make_async_copy(source, target, sem)
        copy.start()
        copy.wait()

    def combine(g, is_near, place):
        view = stage.reshape(2, 8, 48, WIDE).at[:, :, :, pl.ds(0, HALF[g])]

        @pl.loop(0, 2)
        def _(pair):
            ahead = 1 - 2 * pair
            codes = column_codes(g, is_near, pair)
            scale = jnp.concatenate(
                [meta_of(g, is_near, pair, i, k)[TOPK:] for i in range(2) for k in range(2)], axis=1
            )
            for side, by in enumerate((0, ahead if is_near else -ahead)):
                rows = pattern[g] + line_base(g, by)
                total = jnp.where(rows == codes[0:1], scale[0:1], 0.0)
                for k in range(1, TOPK):
                    total = jnp.where(rows == codes[k : k + 1], scale[k : k + 1], total)
                share[:, side * 384 : (side + 1) * 384] = total.T.astype(jnp.bfloat16)
            await_bytes(backbox[g].at[int(is_near), pair], back_recv.at[g, int(is_near), pair])
            load(backbox[g].at[int(is_near), pair], view, stage_sem.at[0])
            if not is_near:
                await_bytes(landed[g].at[pair], sum_recv.at[g, pair])
                load(landed[g].at[pair], low.at[:, :, :, pl.ds(0, HALF[g])], stage_sem.at[1])
            for low_at, size in tiles(HALF[g]):
                block = stage[:, :, :, :, low_at : low_at + size].reshape(768, size)
                mixed = jnp.dot(share[...], block, preferred_element_type=jnp.float32)
                place(pair, low_at, size, mixed.reshape(2, 2, TOK, size))

    def pass_on(g):
        def place(pair, low_at, size, block):
            near[g][pair, :, :, :, low_at : low_at + size] = block.astype(jnp.bfloat16)

        combine(g, True, place)
        for pair in range(2):
            remote(near[g].at[pair], landed[g].at[pair], sum_send.at[g, pair], sum_recv.at[g, pair],
                   moved(at, ROLES[g][1], 2 * pair - 1))

    def own_at(g, chip, half):
        rows = pl.ds(pl.multiple_of((chip * 2 + half) * TOK, TOK), TOK)
        if g == 2:
            return own2, rows, 0
        return acc, rows, g * WIDE

    def settled(g, chip, half):
        ref, rows, column = own_at(g, chip, half)
        return ref[rows, column : column + HALF[g]]

    def home(g):
        axis_a = ROLES[g][0]

        def place(pair, low_at, size, block):
            for i in range(2):
                for half in range(2):
                    ref, rows, column = own_at(g, pair * 2 + i, half)
                    value = block[i, half] + low[i, half, :, low_at : low_at + size].astype(jnp.float32)
                    ref[rows, column + low_at : column + low_at + size] = value

        combine(g, False, place)
        opposite = step_on(at[axis_a], 2)
        for half, by in enumerate((1, -1)):
            gathered[g][0, half] = settled(g, opposite, half).astype(jnp.bfloat16)
            remote(gathered[g].at[0, half], arrived[g].at[half], c_send.at[g, half], c_recv.at[g, half],
                   moved(at, axis_a, by))

    def relay(g):
        axis_a = ROLES[g][0]
        for half_in, by in enumerate((1, -1)):
            a_to = step_on(at[axis_a], by)
            await_bytes(arrived[g].at[half_in], c_recv.at[g, half_in])
            for half in range(2):
                value = settled(g, a_to, half)
                if half == half_in:
                    value = value + arrived[g][half_in].astype(jnp.float32)
                gathered[g][1 + half_in, half] = value.astype(jnp.bfloat16)
            remote(gathered[g].at[1 + half_in], arrived[g].at[pl.ds(2 + 2 * half_in, 2)], c_send.at[g, 2 + half_in],
                   c_recv.at[g, 2 + half_in], moved(at, axis_a, by))

    def finish(g):
        for index in range(2):
            await_bytes(arrived[g].at[pl.ds(2 + 2 * index, 2)], c_recv.at[g, 2 + index])
        for half in range(2):
            value = settled(g, at[ROLES[g][0]], half) + arrived[g][2 + half].astype(jnp.float32)
            value = value + arrived[g][4 + half].astype(jnp.float32)
            last[half, :, START[g] // 2 : START[g] // 2 + HALF[g]] = value.astype(jnp.bfloat16)
        span = pl.ds(START[g] // 2, HALF[g])
        remote(last.at[other, :, span], ends[g], end_send.at[g], end_recv.at[g], moved(at, "x", 0, other))

    for order in (3, 1, 2, 0):
        for g in groups:
            expand_and_send(g, order)
    for g in groups:
        pass_on(g)
    for g in groups:
        for way in range(2):
            await_bytes(gathered[g].at[0], a_send.at[g, way])
            await_bytes(gathered[g].at[0, 0], ah_send.at[g, way])
        for order in range(4):
            await_bytes(gathered[g].at[0], b_send.at[g, order])
    home(0)
    home(1)
    relay(0)
    home(2)
    relay(1)
    relay(2)
    for g in groups:
        finish(g)
    for g in groups:
        mine = last[core, :, START[g] // 2 : START[g] // 2 + HALF[g]]
        await_bytes(ends[g], end_recv.at[g])
        theirs = ends[g][...]
        result[:, START[g] : START[g] + HALF[g]] = jnp.where(core == 0, mine, theirs)
        result[:, START[g] + HALF[g] : START[g] + WIDTH[g]] = jnp.where(core == 0, theirs, mine)
    for g in groups:
        await_bytes(metas[g].at[0, 0], meta_send.at[g, 0])
        await_bytes(metas[g].at[pl.ds(0, 3)], meta_send.at[g, 1])
        await_bytes(near_metas[g], meta_send.at[g, 2])
        await_bytes(staged[g].at[0], core_send.at[g])
        for order in range(4):
            for pair in range(2):
                count = 7 if RETURNS[order, pair][1] == 0 else 8
                await_bytes(outbox[g].at[0, pl.ds(0, count)], back_send.at[g, order, pair])
        for index in range(2):
            await_bytes(near[g].at[index], sum_send.at[g, index])
            await_bytes(arrived[g].at[index], c_send.at[g, index])
            await_bytes(arrived[g].at[pl.ds(0, 2)], c_send.at[g, 2 + index])
        await_bytes(ends[g], end_send.at[g])


def row_pattern():
    row = np.arange(384)
    line, core, inner = row // 96, row // 48 % 2, row % 48
    tables = []
    for roles in ROLES:
        spot = {"x": 0 * line, "y": 0 * line, "z": 0 * line, "core": core}
        spot[roles[2]] = line
        node, local = device(spot)
        tables.append(((node * 8 + local) * SLOTS + inner % SLOTS) * 4 + inner // SLOTS)
    return jnp.asarray(np.stack(tables)[:, :, None].astype(np.float32))


def body(tokens, norm_gain, routes, route_gates, placement, gate_weight, up_weight, down_weight):
    experts = placement.shape[0]
    blocks = TOK // BLOCK_TOK
    bf16, f32 = jnp.bfloat16, jnp.float32
    combine_weight = (route_gates / jnp.sum(route_gates, axis=-1, keepdims=True)).astype(bf16)
    expert_ids = jnp.arange(experts, dtype=jnp.int32)
    holder = jnp.sum(jnp.where(placement[None, :] == expert_ids[:, None], expert_ids[None, :], 0), axis=1)
    one_hot = routes[:, :, None] == expert_ids
    target = jnp.sum(jnp.where(one_hot, holder, 0), axis=-1)
    named = jnp.any(one_hot, axis=1).astype(f32).reshape(blocks, BLOCK_TOK, experts)
    before = jnp.einsum("ts,bse->bte", jnp.tril(jnp.ones((BLOCK_TOK, BLOCK_TOK), f32), -1), named)
    position_in = jnp.sum(jnp.where(one_hot, before.reshape(TOK, 1, experts), 0.0), axis=-1)
    block = (jnp.arange(TOK) // BLOCK_TOK).astype(f32)[:, None]
    code = target.astype(f32) * SLOTS + block * CAP + position_in
    own_meta = jnp.concatenate([code.T, combine_weight.astype(f32).T], axis=0)

    vmem, hbm = pl.BlockSpec(memory_space=pltpu.VMEM), pl.BlockSpec(memory_space=pltpu.HBM)
    dma = pltpu.SemaphoreType.DMA
    shape = jax.ShapeDtypeStruct
    meta = (2, 2 * TOPK, TOK)

    def each(*dims):
        return [pltpu.VMEM((*dims, h), bf16) for h in HALF]

    result, *_ = pl.pallas_call(
        kernel,
        out_shape=[shape((TOK, D), bf16)]
        + [shape((4, 2, SIDE, 2, 48, h), bf16) for h in HALF]
        + [shape((2, 2, 2, 8, 48, h), bf16) for h in HALF]
        + [shape((2, 2, 2, TOK, h), bf16) for h in HALF],
        in_specs=[vmem] * 4 + [hbm] * 3,
        out_specs=[vmem] + [hbm] * 9,
        scratch_shapes=each(SIDE, 2, TOK)
        + each(2, 2, 2, TOK)
        + each(8, 8, 48)
        + each(2, TOK)
        + [pltpu.VMEM((SIDE, *meta), f32)] * 3
        + [pltpu.VMEM((2, 2, *meta), f32)] * 3
        + [
            pltpu.VMEM((2, SIDE, 2, 48, WIDE), bf16),
            pltpu.VMEM((512, 768), bf16),
            pltpu.VMEM((384, HID), bf16),
            pltpu.VMEM((D, 2 * HID), bf16),
            pltpu.VMEM((64 * UNIT, 2 * HID), f32),
            pltpu.VMEM((SIDE * 2 * TOK, HALF[2]), f32),
            pltpu.VMEM((2, 2, TOK, WIDE), bf16),
        ]
        + each(6, TOK)
        + [pltpu.VMEM((2, TOK, D // 2), bf16)]
        + each(TOK)
        + [
            dma((5,)), dma((3,)), dma((3,)), dma((3,)), dma((3, 3)), dma((3, 3)),
            dma((3, 2)), dma((3, 2)), dma((3, 2)), dma((3, 2)), dma((3, 4)), dma((3, 2)),
            dma((3, 4)), dma((3, 4)), dma((2,)), dma((3, 4, 2)), dma((3, 2, 2)), dma((3, 2)), dma((3, 2)),
            dma((3, 4)), dma((3, 4)), dma((3,)), dma((3,)),
        ],
        compiler_params=pltpu.CompilerParams(collective_id=0, has_side_effects=True, vmem_limit_bytes=VMEM_LIMIT),
        name="experts",
    )(tokens, norm_gain[None, :], own_meta, row_pattern(), gate_weight, up_weight, down_weight)
    return result


def solution(mesh):
    rows = P(("node", "local"), None)
    whole = P(("node", "local"), None, None)
    in_specs = (rows, P(), rows, rows, P(), whole, whole, whole)
    return jax.shard_map(body, mesh=mesh, in_specs=in_specs, out_specs=rows, check_vma=False)
```

```python
import jax
import jax.numpy as jnp
import numpy as np
from jax import lax
from jax.experimental import pallas as pl
from jax.experimental.pallas import tpu as pltpu
from jax.sharding import PartitionSpec as P

MESH = pl.DeviceIdType.MESH
BLOCK_TOK = 32
CAP = 3
EPSILON = 1e-06
SIDE = 4
TOK = 128
TOPK = 8
D = 4096
HID = 768
SLOTS = 12
UNIT = 2 * SLOTS
ROLES = (("x", "y", "z"), ("y", "z", "x"), ("z", "x", "y"))
WIDTH = (1536, 1280, 1280)
START = (0, 1536, 2816)
HALF = tuple(w // 2 for w in WIDTH)
WIDE = max(HALF)
STRIDE = {"x": 16, "y": 4, "z": 1}
STEPS = (0, -1, 1, 2)
RETURNS = {
    (0, 0): (0, 0), (0, 1): (0, 0),
    (1, 0): (2, 0), (1, 1): (1, -1),
    (2, 0): (1, 1), (2, 1): (2, 0),
    (3, 0): (3, -1), (3, 1): (3, 1),
}
VMEM_LIMIT = 62 << 20


def position():
    node, local = lax.axis_index("node"), lax.axis_index("local")
    return {
        "x": (node // 2) % 2 * 2 + local % 2,
        "y": node // 4,
        "z": local // 2,
        "core": node % 2,
    }


def device(at):
    node = (at["y"] * 2 + at["x"] // 2) * 2 + at["core"]
    return node, at["z"] * 2 + at["x"] % 2


def step_on(value, by):
    return (value + by + SIDE) % SIDE


def moved(at, axis, by, core=None, axis2=None, by2=0):
    new = dict(at)
    new[axis] = step_on(at[axis], by)
    if axis2 is not None:
        new[axis2] = step_on(at[axis2], by2)
    if core is not None:
        new["core"] = core
    return device(new)


def greet(at, barrier):
    other = 1 - at["core"]
    partners = [moved(at, "x", 0, other)]
    for _, axis_b, axis_c in ROLES:
        for by in (1, -1, 2):
            for core in (at["core"], other):
                partners.append(moved(at, axis_c, by, core))
                for side in (1, -1):
                    partners.append(moved(at, axis_c, by, core, axis_b, side))
    for partner in partners:
        pl.semaphore_signal(barrier, inc=1, device_id=partner, device_id_type=MESH)
    return len(partners)


def remote(src, dst, send, recv, target):
    pltpu.make_async_remote_copy(
        src_ref=src, dst_ref=dst, send_sem=send, recv_sem=recv, device_id=target, device_id_type=MESH
    ).start()


def local_copy(src, dst, sem):
    pltpu.make_async_copy(src, dst, sem).start()


def await_bytes(ref, sem):
    pltpu.make_async_copy(ref, ref, sem).wait()


def tiles(width):
    return [(at, min(256, width - at)) for at in range(0, width, 256)]


def slot_codes(routes, packed, placement):
    side = (TOK, TOK)
    down = lax.broadcasted_iota(jnp.int32, side, 0)
    across = lax.broadcasted_iota(jnp.int32, side, 1)
    earlier = jnp.logical_and(down < across, down // BLOCK_TOK == across // BLOCK_TOK)
    place = jnp.broadcast_to(placement[...].astype(jnp.float32), side).T
    index = down.astype(jnp.float32)
    columns = [jnp.broadcast_to(routes[:, k : k + 1].astype(jnp.float32), side) for k in range(TOPK)]
    block = (across[0:1] // BLOCK_TOK * CAP).astype(jnp.float32)
    codes = []
    for k in range(TOPK):
        wanted = packed[k : k + 1]
        holder = jnp.sum(jnp.where(place == wanted, index, 0.0), axis=0, keepdims=True)
        same = columns[0] == wanted
        for column in columns[1:]:
            same = jnp.logical_or(same, column == wanted)
        count = jnp.sum(jnp.where(jnp.logical_and(same, earlier), 1.0, 0.0), axis=0, keepdims=True)
        codes.append(holder * float(SLOTS) + block + count)
    gates = packed[TOPK:]
    weight = gates / jnp.sum(gates, axis=0, keepdims=True)
    return jnp.concatenate(codes + [weight.astype(jnp.bfloat16).astype(jnp.float32)], axis=0)


def kernel(
    tokens, gain, routes, packed, placement, lines, gate_w, up_w, down_w,
    result, in0, in1, in2, back0, back1, back2, land0, land1, land2,
    g0, g1, g2, n0, n1, n2, out0, out1, out2, st0, st1, st2, m0, m1, m2, k0, k1, k2,
    code_box, stage, share, rows_bf, weights, acc, own2, low, r0, r1, r2, last, end0, end1, end2,
    w_sem, own_sem, core_send, core_recv, meta_send, meta_recv, a_send, a_recv, ah_send, ah_recv, b_send, b_recv,
    row_send, row_recv, stage_sem, back_send, back_recv, sum_send, sum_recv, c_send, c_recv, end_send, end_recv,
):
    at = position()
    core = at["core"]
    other = 1 - core
    groups = range(3)
    gathered, near, outbox, inbox = (g0, g1, g2), (n0, n1, n2), (out0, out1, out2), (in0, in1, in2)
    staged, metas, near_metas = (st0, st1, st2), (m0, m1, m2), (k0, k1, k2)
    backbox, landed, arrived, ends = (back0, back1, back2), (land0, land1, land2), (r0, r1, r2), (end0, end1, end2)
    barrier = pltpu.get_barrier_semaphore()
    greeted = greet(at, barrier)
    local_copy(gate_w.at[0], weights.at[:, pl.ds(0, HID)], w_sem.at[0])
    local_copy(up_w.at[0], weights.at[:, pl.ds(HID, HID)], w_sem.at[1])

    @pl.loop(0, TOK // 16)
    def _(step):
        rows = pl.ds(pl.multiple_of(step * 16, 16), 16)
        values = tokens[rows, :].astype(jnp.float32)
        rescale = lax.rsqrt(jnp.sum(values * values, axis=-1, keepdims=True) * (1.0 / D) + EPSILON)
        normed = (values * rescale * gain[...].astype(jnp.float32)).astype(jnp.bfloat16)
        for g in groups:
            for h in range(2):
                low_at = START[g] + h * HALF[g]
                staged[g][h, rows, :] = normed[:, low_at : low_at + HALF[g]]

    pl.semaphore_wait(barrier, greeted)
    for g in groups:
        a = at[ROLES[g][0]]
        remote(staged[g].at[other], gathered[g].at[a, core], core_send.at[g], core_recv.at[g], moved(at, "x", 0, other))
        local_copy(staged[g].at[core], gathered[g].at[a, core], own_sem.at[g])

    def ring(g, half, first):
        axis_a = ROLES[g][0]
        a = at[axis_a]
        source = staged[g].at[half] if first else gathered[g].at[a, half]
        for way, by in enumerate((1, -1)):
            remote(source, gathered[g].at[a, half], a_send.at[g, way, half], a_recv.at[g, way, half], moved(at, axis_a, by))

    def spread_own(g, half, first):
        a = at[ROLES[g][0]]
        pair = a // 2
        source = staged[g].at[half] if first else gathered[g].at[a, half]
        remote(source, near[g].at[pair, a % 2, half], b_send.at[g, 0 if first else 4], b_recv.at[g, pair],
               moved(at, ROLES[g][1], 1 - 2 * pair))

    def spread(g, order, a_from):
        pair = a_from // 2
        remote(gathered[g].at[a_from], near[g].at[pair, a_from % 2], b_send.at[g, order], b_recv.at[g, pair],
               moved(at, ROLES[g][1], 1 - 2 * pair))

    for g in groups:
        ring(g, core, True)
    for g in groups:
        spread_own(g, core, True)
    code_box[...] = slot_codes(routes, packed, placement)
    for g in groups:
        a = at[ROLES[g][0]]
        metas[g][a, core] = code_box[...]
        remote(code_box, metas[g].at[a, core], meta_send.at[g, 0], meta_recv.at[g, 0], moved(at, "x", 0, other))
    for g in groups:
        await_bytes(staged[g].at[0], core_recv.at[g])
        ring(g, other, False)
    for g in groups:
        spread_own(g, other, False)
    for g in groups:
        axis_a = ROLES[g][0]
        a = at[axis_a]
        await_bytes(code_box, meta_recv.at[g, 0])
        for by in (1, -1, 2):
            remote(metas[g].at[a], metas[g].at[a], meta_send.at[g, 1], meta_recv.at[g, 1], moved(at, axis_a, by))

    @pl.loop(0, 64)
    def _(unit):
        acc[pl.ds(pl.multiple_of(unit * UNIT, 8), UNIT), :] = jnp.zeros((UNIT, 2 * HID), jnp.float32)

    for way, by in enumerate((1, -1)):
        for g in groups:
            axis_a = ROLES[g][0]
            a_from = step_on(at[axis_a], -by)
            await_bytes(gathered[g].at[a_from, way], a_recv.at[g, way, way])
            remote(gathered[g].at[a_from, way], gathered[g].at[a_from, way], ah_send.at[g, way], ah_recv.at[g, way],
                   moved(at, axis_a, by))
    for way, by in enumerate((1, -1)):
        for g in groups:
            a_from = step_on(at[ROLES[g][0]], -by)
            await_bytes(gathered[g].at[a_from, 1 - way], a_recv.at[g, way, 1 - way])
            spread(g, 1 + way, a_from)
    for g in groups:
        await_bytes(metas[g].at[pl.ds(0, 3)], meta_recv.at[g, 1])
        for pair in range(2):
            remote(metas[g].at[pl.ds(2 * pair, 2)], near_metas[g].at[pair], meta_send.at[g, 2], meta_recv.at[g, 2],
                   moved(at, ROLES[g][1], 1 - 2 * pair))
    for g in groups:
        await_bytes(gathered[g].at[0, 0], own_sem.at[g])
        a_from = step_on(at[ROLES[g][0]], 2)
        for way in range(2):
            await_bytes(gathered[g].at[a_from, way], ah_recv.at[g, way])
        spread(g, 3, a_from)

    def line_base(g, by):
        _, axis_b, axis_c = ROLES[g]
        spot = dict(at)
        spot[axis_b] = step_on(at[axis_b], by)
        spot[axis_c] = 0
        spot["core"] = 0
        node, local = device(spot)
        return ((node * 8 + local) * SLOTS).astype(jnp.float32)

    def meta_of(g, is_near, pair, index, k):
        return near_metas[g][pair, index, k] if is_near else metas[g][pair * 2 + index, k]

    def slot_rows(g, is_near, pair, index, by):
        both = [meta_of(g, is_near, pair, index, k) for k in range(2)]
        table = jnp.concatenate(both, axis=1)
        first = lines[g] + line_base(g, by)
        slot = jnp.full((8, 2 * TOK), -100.0, jnp.float32)
        weight = jnp.zeros((8, 2 * TOK), jnp.float32)
        for k in range(TOPK):
            offset = table[k : k + 1] - first
            hit = jnp.logical_and(offset >= 0.0, offset < float(SLOTS))
            slot = jnp.where(hit, offset, slot)
            weight = jnp.where(hit, table[TOPK + k : TOPK + k + 1], weight)
        lane = lax.broadcasted_iota(jnp.int32, (8, 2 * TOK), 1)
        return slot + jnp.where(lane >= TOK, float(SLOTS), 0.0), weight

    def pick_and_send(g, kind):
        _, axis_b, axis_c = ROLES[g]
        is_near = kind >= 2

        @pl.loop(0, 2)
        def _(pair):
            if kind == 3:
                await_bytes(near[g].at[pair], b_recv.at[g, pair])
            ahead = 1 - 2 * pair
            by_b = (0, -ahead, 0, ahead)[kind]
            order = (0, 2 - pair, 1 + pair, 3)[kind]
            number = lax.broadcasted_iota(jnp.int32, (UNIT, 2 * TOK), 0).astype(jnp.float32)
            for i in range(2):
                slot, _ = slot_rows(g, is_near, pair, i, by_b)
                found = [jnp.where(number == slot[d : d + 1], 1.0, 0.0) for d in range(8)]
                share[0 : 8 * UNIT, i * 256 : (i + 1) * 256] = jnp.concatenate(found, axis=0).astype(jnp.bfloat16)
            for low_at, size in tiles(HALF[g]):
                span = slice(low_at, low_at + size)
                parts = []
                for i in range(2):
                    block = near[g][pair, i, :, :, span] if is_near else gathered[g][pair * 2 + i, :, :, span]
                    picked = jnp.dot(share[0 : 8 * UNIT, i * 256 : (i + 1) * 256], block.reshape(2 * TOK, size),
                                     preferred_element_type=jnp.float32)
                    parts.append(picked.reshape(8, UNIT, size))
                outbox[g][kind * 2 + pair, :, :, span] = jnp.concatenate(parts, axis=1).astype(jnp.bfloat16)
            c = at[axis_c]
            for by in (1, -1, 2, 0):
                c_to = step_on(c, by)
                for k in range(2):
                    core_to = (core + k) % 2
                    box = outbox[g].at[kind * 2 + pair, c_to * 2 + core_to]
                    slot = inbox[g].at[order, core, c, pair]
                    if by == 0 and k == 0 and kind in (0, 2):
                        local_copy(box, slot, row_recv.at[g, order])
                    else:
                        remote(box, slot, row_send.at[g, kind], row_recv.at[g, order],
                               moved(at, axis_c, by, core_to, axis_b, by_b))

    def bring(g, order):
        await_bytes(inbox[g].at[order], row_recv.at[g, order])
        local_copy(inbox[g].at[order], stage.at[g % 2, :, :, :, :, pl.ds(0, HALF[g])], stage_sem.at[g % 2])

    def multiply(g, order):
        axis_a, axis_b, axis_c = ROLES[g]
        b_from = step_on(at[axis_b], STEPS[order])
        await_bytes(stage.at[g % 2, :, :, :, :, pl.ds(0, HALF[g])], stage_sem.at[g % 2])

        @pl.loop(0, 2 * HID // 256)
        def _(tile):
            columns = pl.ds(pl.multiple_of(tile * 256, 256), 256)
            total = None
            for h in range(2):
                rows = stage[g % 2, h, :, :, :, 0 : HALF[g]].reshape(384, HALF[g])
                part = jnp.dot(rows, weights[START[g] + h * HALF[g] : START[g] + (h + 1) * HALF[g], columns],
                               preferred_element_type=jnp.float32)
                total = part if total is None else total + part
            for c in range(SIDE):
                for a in range(SIDE):
                    unit = a * STRIDE[axis_a] + b_from * STRIDE[axis_b] + c * STRIDE[axis_c]
                    low_at = (c * SIDE + a) * UNIT
                    acc[pl.ds(pl.multiple_of(unit * UNIT, 8), UNIT), columns] += total[low_at : low_at + UNIT]

    for kind in (0, 1):
        for g in groups:
            pick_and_send(g, kind)
    for g in groups:
        await_bytes(near_metas[g], meta_recv.at[g, 2])
    for kind in (3, 2):
        for g in groups:
            pick_and_send(g, kind)
    await_bytes(weights.at[:, pl.ds(0, HID)], w_sem.at[0])
    await_bytes(weights.at[:, pl.ds(HID, HID)], w_sem.at[1])

    def down_of(g):
        return weights.at[pl.ds(g * HID, HID), pl.ds(0, WIDTH[g])]

    def fetch_down(g):
        local_copy(down_w.at[0, :, pl.ds(START[g], WIDTH[g])], down_of(g), w_sem.at[2 + g])

    for order in (0, 3, 1, 2):
        bring(0, order)
        for g in groups:
            if g < 2:
                bring(g + 1, order)
            multiply(g, order)
            if order == 2 and g == 0:
                fetch_down(0)
                fetch_down(1)
            if order == 2 and g == 1:
                fetch_down(2)

    @pl.loop(0, 64)
    def _(unit):
        rows = pl.ds(pl.multiple_of(unit * UNIT, 8), UNIT)
        gate, up = acc[rows, 0:HID], acc[rows, HID : 2 * HID]
        hidden = gate / (1.0 + jnp.exp(-gate)) * up
        acc[rows, 0:HID] = hidden.astype(jnp.bfloat16).astype(jnp.float32)

    for g in groups:
        for kind in range(4):
            count = 7 if kind in (0, 2) else 8
            await_bytes(outbox[g].at[pl.ds(0, 2), pl.ds(0, count)], row_send.at[g, kind])
    for g in groups:
        await_bytes(down_of(g), w_sem.at[2 + g])

    def expand_and_send(g, order):
        axis_a, axis_b, axis_c = ROLES[g]
        b_to = step_on(at[axis_b], STEPS[order])
        for c in range(SIDE):
            units = [
                acc[pl.ds(pl.multiple_of(
                    (a * STRIDE[axis_a] + b_to * STRIDE[axis_b] + c * STRIDE[axis_c]) * UNIT, 8), UNIT), 0:HID]
                for a in range(SIDE)
            ]
            rows_bf[c * 96 : (c + 1) * 96, :] = jnp.concatenate(units, axis=0).astype(jnp.bfloat16)

        c = at[axis_c]
        for k in range(2):
            core_to = (core + k) % 2
            for low_at, size in tiles(HALF[g]):
                columns = pl.ds(pl.multiple_of(core_to * HALF[g] + low_at, 128), size)
                made = jnp.dot(rows_bf[...], weights[g * HID : (g + 1) * HID, columns], preferred_element_type=jnp.float32)
                made = made.astype(jnp.bfloat16).reshape(SIDE, 2, 48, size)
                for pair in range(2):
                    outbox[g][order * 2 + pair, pl.ds(core_to * SIDE, SIDE), :, low_at : low_at + size] = made[:, pair]
            for pair in range(2):
                kind, by_b = RETURNS[order, pair]
                for by in (1, -1, 2, 0):
                    c_to = step_on(c, by)
                    box = outbox[g].at[order * 2 + pair, core_to * SIDE + c_to]
                    slot = backbox[g].at[kind // 2, pair, kind % 2, c * 2 + core]
                    sem = back_recv.at[g, kind // 2, pair]
                    if by == 0 and k == 0 and by_b == 0:
                        local_copy(box, slot, sem)
                    else:
                        remote(box, slot, back_send.at[g, order, pair], sem, moved(at, axis_c, by, core_to, axis_b, by_b))

    def combine(g, is_near, place):
        wide = pl.ds(0, HALF[g])
        views = stage.reshape(2, 2, 8, 48, WIDE).at[:, :, :, :, wide]
        for pair in range(2):
            await_bytes(backbox[g].at[int(is_near), pair], back_recv.at[g, int(is_near), pair])
            local_copy(backbox[g].at[int(is_near), pair], views.at[pair], stage_sem.at[pair])
            if not is_near:
                await_bytes(landed[g].at[pair], sum_recv.at[g, pair])
                local_copy(landed[g].at[pair], low.at[pair, :, :, :, wide], stage_sem.at[2 + pair])

        @pl.loop(0, 2)
        def _(pair):
            ahead = 1 - 2 * pair
            number = lax.broadcasted_iota(jnp.int32, (48, 2 * TOK), 0).astype(jnp.float32)
            for side, by in enumerate((0, ahead if is_near else -ahead)):
                for i in range(2):
                    slot, weight = slot_rows(g, is_near, pair, i, by)
                    slot = slot + float(i * UNIT)
                    found = [jnp.where(number == slot[d : d + 1], weight[d : d + 1], 0.0) for d in range(8)]
                    total = jnp.concatenate(found, axis=0).T.astype(jnp.bfloat16)
                    share[i * 256 : (i + 1) * 256, side * 384 : (side + 1) * 384] = total
            await_bytes(views.at[pair], stage_sem.at[pair])
            if not is_near:
                await_bytes(low.at[pair, :, :, :, wide], stage_sem.at[2 + pair])
            for low_at, size in tiles(HALF[g]):
                block = stage[pair, :, :, :, :, low_at : low_at + size].reshape(768, size)
                mixed = jnp.dot(share[...], block, preferred_element_type=jnp.float32)
                place(pair, low_at, size, mixed.reshape(2, 2, TOK, size))

    def pass_on(g):
        def place(pair, low_at, size, block):
            near[g][pair, :, :, :, low_at : low_at + size] = block.astype(jnp.bfloat16)

        combine(g, True, place)
        for pair in range(2):
            remote(near[g].at[pair], landed[g].at[pair], sum_send.at[g, pair], sum_recv.at[g, pair],
                   moved(at, ROLES[g][1], 2 * pair - 1))

    def own_at(g, chip, half):
        rows = pl.ds(pl.multiple_of((chip * 2 + half) * TOK, TOK), TOK)
        if g == 2:
            return own2, rows, 0
        return acc, rows, g * WIDE

    def settled(g, chip, half):
        ref, rows, column = own_at(g, chip, half)
        return ref[rows, column : column + HALF[g]]

    def home(g):
        axis_a = ROLES[g][0]

        def place(pair, low_at, size, block):
            for i in range(2):
                for half in range(2):
                    ref, rows, column = own_at(g, pair * 2 + i, half)
                    value = block[i, half] + low[pair, i, half, :, low_at : low_at + size].astype(jnp.float32)
                    ref[rows, column + low_at : column + low_at + size] = value

        combine(g, False, place)
        opposite = step_on(at[axis_a], 2)
        for half, by in enumerate((1, -1)):
            gathered[g][0, half] = settled(g, opposite, half).astype(jnp.bfloat16)
            remote(gathered[g].at[0, half], arrived[g].at[half], c_send.at[g, half], c_recv.at[g, half],
                   moved(at, axis_a, by))

    def relay(g):
        axis_a = ROLES[g][0]
        for half_in, by in enumerate((1, -1)):
            a_to = step_on(at[axis_a], by)
            await_bytes(arrived[g].at[half_in], c_recv.at[g, half_in])
            for half in range(2):
                value = settled(g, a_to, half)
                if half == half_in:
                    value = value + arrived[g][half_in].astype(jnp.float32)
                gathered[g][1 + half_in, half] = value.astype(jnp.bfloat16)
            remote(gathered[g].at[1 + half_in], arrived[g].at[pl.ds(2 + 2 * half_in, 2)], c_send.at[g, 2 + half_in],
                   c_recv.at[g, 2 + half_in], moved(at, axis_a, by))

    def finish(g):
        for index in range(2):
            await_bytes(arrived[g].at[pl.ds(2 + 2 * index, 2)], c_recv.at[g, 2 + index])
        for half in range(2):
            value = settled(g, at[ROLES[g][0]], half) + arrived[g][2 + half].astype(jnp.float32)
            value = value + arrived[g][4 + half].astype(jnp.float32)
            last[half, :, START[g] // 2 : START[g] // 2 + HALF[g]] = value.astype(jnp.bfloat16)
        span = pl.ds(START[g] // 2, HALF[g])
        remote(last.at[other, :, span], ends[g], end_send.at[g], end_recv.at[g], moved(at, "x", 0, other))

    for order in (3, 1, 2, 0):
        for g in groups:
            expand_and_send(g, order)
    for g in groups:
        pass_on(g)
    for g in groups:
        for way in range(2):
            for half in range(2):
                await_bytes(gathered[g].at[0, 0], a_send.at[g, way, half])
            await_bytes(gathered[g].at[0, 0], ah_send.at[g, way])
        for order in range(5):
            await_bytes(gathered[g].at[0] if order in (1, 2, 3) else gathered[g].at[0, 0], b_send.at[g, order])
    home(0)
    home(1)
    relay(0)
    home(2)
    relay(1)
    relay(2)
    for g in groups:
        finish(g)
    for g in groups:
        mine = last[core, :, START[g] // 2 : START[g] // 2 + HALF[g]]
        await_bytes(ends[g], end_recv.at[g])
        theirs = ends[g][...]
        result[:, START[g] : START[g] + HALF[g]] = jnp.where(core == 0, mine, theirs)
        result[:, START[g] + HALF[g] : START[g] + WIDTH[g]] = jnp.where(core == 0, theirs, mine)
    for g in groups:
        await_bytes(metas[g].at[0, 0], meta_send.at[g, 0])
        await_bytes(metas[g].at[pl.ds(0, 3)], meta_send.at[g, 1])
        await_bytes(near_metas[g], meta_send.at[g, 2])
        await_bytes(staged[g].at[0], core_send.at[g])
        for order in range(4):
            for pair in range(2):
                count = 7 if RETURNS[order, pair][1] == 0 else 8
                await_bytes(outbox[g].at[0, pl.ds(0, count)], back_send.at[g, order, pair])
        for index in range(2):
            await_bytes(near[g].at[index], sum_send.at[g, index])
            await_bytes(arrived[g].at[index], c_send.at[g, index])
            await_bytes(arrived[g].at[pl.ds(0, 2)], c_send.at[g, 2 + index])
        await_bytes(ends[g], end_send.at[g])


def line_table():
    expert = np.arange(8)
    tables = []
    for roles in ROLES:
        spot = {"x": 0 * expert, "y": 0 * expert, "z": 0 * expert, "core": expert % 2}
        spot[roles[2]] = expert // 2
        node, local = device(spot)
        tables.append((node * 8 + local) * SLOTS)
    return jnp.asarray(np.stack(tables)[:, :, None].astype(np.float32))


def body(tokens, norm_gain, routes, route_gates, placement, gate_weight, up_weight, down_weight):
    bf16, f32 = jnp.bfloat16, jnp.float32
    packed = jnp.concatenate([routes.astype(f32), route_gates], axis=1).T

    vmem, hbm = pl.BlockSpec(memory_space=pltpu.VMEM), pl.BlockSpec(memory_space=pltpu.HBM)
    dma = pltpu.SemaphoreType.DMA
    shape = jax.ShapeDtypeStruct
    meta = (2, 2 * TOPK, TOK)

    def each(*dims):
        return [pltpu.VMEM((*dims, h), bf16) for h in HALF]

    result, *_ = pl.pallas_call(
        kernel,
        out_shape=[shape((TOK, D), bf16)]
        + [shape((4, 2, SIDE, 2, 48, h), bf16) for h in HALF]
        + [shape((2, 2, 2, 8, 48, h), bf16) for h in HALF]
        + [shape((2, 2, 2, TOK, h), bf16) for h in HALF],
        in_specs=[vmem] * 6 + [hbm] * 3,
        out_specs=[vmem] + [hbm] * 9,
        scratch_shapes=each(SIDE, 2, TOK)
        + each(2, 2, 2, TOK)
        + each(8, 8, 48)
        + each(2, TOK)
        + [pltpu.VMEM((SIDE, *meta), f32)] * 3
        + [pltpu.VMEM((2, 2, *meta), f32)] * 3
        + [
            pltpu.VMEM((2 * TOPK, TOK), f32),
            pltpu.VMEM((2, 2, SIDE, 2, 48, WIDE), bf16),
            pltpu.VMEM((512, 768), bf16),
            pltpu.VMEM((384, HID), bf16),
            pltpu.VMEM((D, 2 * HID), bf16),
            pltpu.VMEM((64 * UNIT, 2 * HID), f32),
            pltpu.VMEM((SIDE * 2 * TOK, HALF[2]), f32),
            pltpu.VMEM((2, 2, 2, TOK, WIDE), bf16),
        ]
        + each(6, TOK)
        + [pltpu.VMEM((2, TOK, D // 2), bf16)]
        + each(TOK)
        + [
            dma((5,)), dma((3,)), dma((3,)), dma((3,)), dma((3, 3)), dma((3, 3)),
            dma((3, 2, 2)), dma((3, 2, 2)), dma((3, 2)), dma((3, 2)), dma((3, 5)), dma((3, 2)),
            dma((3, 4)), dma((3, 4)), dma((4,)), dma((3, 4, 2)), dma((3, 2, 2)), dma((3, 2)), dma((3, 2)),
            dma((3, 4)), dma((3, 4)), dma((3,)), dma((3,)),
        ],
        compiler_params=pltpu.CompilerParams(collective_id=0, has_side_effects=True, vmem_limit_bytes=VMEM_LIMIT),
        name="experts",
    )(tokens, norm_gain[None, :], routes, packed, placement[None, :], line_table(), gate_weight, up_weight, down_weight)
    return result


def solution(mesh):
    rows = P(("node", "local"), None)
    whole = P(("node", "local"), None, None)
    in_specs = (rows, P(), rows, rows, P(), whole, whole, whole)
    return jax.shard_map(body, mesh=mesh, in_specs=in_specs, out_specs=rows, check_vma=False)
```

```python
import jax
import jax.numpy as jnp
import numpy as np
from jax import lax
from jax.experimental import pallas as pl
from jax.experimental.pallas import tpu as pltpu
from jax.sharding import PartitionSpec as P

MESH = pl.DeviceIdType.MESH
BLOCK_TOK = 32
CAP = 3
EPSILON = 1e-06
SIDE = 4
TOK = 128
TOPK = 8
D = 4096
HID = 768
SLOTS = 12
UNIT = 2 * SLOTS
ROLES = (("x", "y", "z"), ("y", "z", "x"), ("z", "x", "y"))
WIDTH = (1536, 1280, 1280)
START = (0, 1536, 2816)
HALF = tuple(w // 2 for w in WIDTH)
WIDE = max(HALF)
STRIDE = {"x": 16, "y": 4, "z": 1}
STEPS = (0, -1, 1, 2)
RETURNS = {
    (0, 0): (0, 0), (0, 1): (0, 0),
    (1, 0): (2, 0), (1, 1): (1, -1),
    (2, 0): (1, 1), (2, 1): (2, 0),
    (3, 0): (3, -1), (3, 1): (3, 1),
}
VMEM_LIMIT = 62 << 20
MIX = 768
EXP = 768


def position():
    node, local = lax.axis_index("node"), lax.axis_index("local")
    return {
        "x": (node // 2) % 2 * 2 + local % 2,
        "y": node // 4,
        "z": local // 2,
        "core": node % 2,
    }


def device(at):
    node = (at["y"] * 2 + at["x"] // 2) * 2 + at["core"]
    return node, at["z"] * 2 + at["x"] % 2


def step_on(value, by):
    return (value + by + SIDE) % SIDE


def moved(at, axis, by, core=None, axis2=None, by2=0):
    new = dict(at)
    new[axis] = step_on(at[axis], by)
    if axis2 is not None:
        new[axis2] = step_on(at[axis2], by2)
    if core is not None:
        new["core"] = core
    return device(new)


def greet(at, barrier):
    other = 1 - at["core"]
    partners = [moved(at, "x", 0, other)]
    for _, axis_b, axis_c in ROLES:
        for by in (1, -1, 2):
            for core in (at["core"], other):
                partners.append(moved(at, axis_c, by, core))
                for side in (1, -1):
                    partners.append(moved(at, axis_c, by, core, axis_b, side))
    for partner in partners:
        pl.semaphore_signal(barrier, inc=1, device_id=partner, device_id_type=MESH)
    return len(partners)


def remote(src, dst, send, recv, target):
    pltpu.make_async_remote_copy(
        src_ref=src, dst_ref=dst, send_sem=send, recv_sem=recv, device_id=target, device_id_type=MESH
    ).start()


def local_copy(src, dst, sem):
    pltpu.make_async_copy(src, dst, sem).start()


def await_bytes(ref, sem):
    pltpu.make_async_copy(ref, ref, sem).wait()


def mix_tiles(width):
    return [(at, min(MIX, width - at)) for at in range(0, width, MIX)]


def tiles(width):
    return [(at, min(EXP, width - at)) for at in range(0, width, EXP)]


def slot_codes(packed, placement):
    side = (TOK, TOK)
    down = lax.broadcasted_iota(jnp.int32, side, 0)
    across = lax.broadcasted_iota(jnp.int32, side, 1)
    earlier = jnp.logical_and(down < across, down // BLOCK_TOK == across // BLOCK_TOK)
    place = jnp.broadcast_to(placement[...].astype(jnp.float32), side).T
    index = down.astype(jnp.float32)
    columns = [jnp.broadcast_to(packed[:, k : k + 1], side) for k in range(TOPK)]
    table = packed[...].T
    block = (across[0:1] // BLOCK_TOK * CAP).astype(jnp.float32)
    codes = []
    for k in range(TOPK):
        wanted = table[k : k + 1]
        holder = jnp.sum(jnp.where(place == wanted, index, 0.0), axis=0, keepdims=True)
        same = columns[0] == wanted
        for column in columns[1:]:
            same = jnp.logical_or(same, column == wanted)
        count = jnp.sum(jnp.where(jnp.logical_and(same, earlier), 1.0, 0.0), axis=0, keepdims=True)
        codes.append(holder * float(SLOTS) + block + count)
    gates = table[TOPK : 2 * TOPK]
    weight = gates / jnp.sum(gates, axis=0, keepdims=True)
    return jnp.concatenate(codes + [weight.astype(jnp.bfloat16).astype(jnp.float32)], axis=0)


def kernel(
    tokens, gain, packed, placement, lines, gate_w, up_w, down_w,
    result, in0, in1, in2, back0, back1, back2, land0, land1, land2,
    g0, g1, g2, n0, n1, n2, out0, out1, out2, st0, st1, st2, m0, m1, m2, k0, k1, k2,
    code_box, stage, lot, share, rows_bf, weights, acc, own2, low, r0, r1, r2, last, end0, end1, end2,
    w_sem, own_sem, core_send, core_recv, meta_send, meta_recv, a_send, a_recv, ah_send, ah_recv, b_send, b_recv,
    row_send, row_recv, stage_sem, back_send, back_recv, sum_send, sum_recv, c_send, c_recv, end_send, end_recv,
):
    at = position()
    core = at["core"]
    other = 1 - core
    groups = range(3)
    gathered, near, outbox, inbox = (g0, g1, g2), (n0, n1, n2), (out0, out1, out2), (in0, in1, in2)
    staged, metas, near_metas = (st0, st1, st2), (m0, m1, m2), (k0, k1, k2)
    backbox, landed, arrived, ends = (back0, back1, back2), (land0, land1, land2), (r0, r1, r2), (end0, end1, end2)
    barrier = pltpu.get_barrier_semaphore()
    greeted = greet(at, barrier)
    local_copy(gate_w.at[0], weights.at[:, pl.ds(0, HID)], w_sem.at[0])
    local_copy(up_w.at[0], weights.at[:, pl.ds(HID, HID)], w_sem.at[1])

    @pl.loop(0, TOK // 16)
    def _(step):
        rows = pl.ds(pl.multiple_of(step * 16, 16), 16)
        values = tokens[rows, :].astype(jnp.float32)
        rescale = lax.rsqrt(jnp.sum(values * values, axis=-1, keepdims=True) * (1.0 / D) + EPSILON)
        normed = (values * rescale * gain[...].astype(jnp.float32)).astype(jnp.bfloat16)
        for g in groups:
            for h in range(2):
                low_at = START[g] + h * HALF[g]
                staged[g][h, rows, :] = normed[:, low_at : low_at + HALF[g]]

    pl.semaphore_wait(barrier, greeted)
    for g in groups:
        a = at[ROLES[g][0]]
        remote(staged[g].at[other], gathered[g].at[a, core], core_send.at[g], core_recv.at[g], moved(at, "x", 0, other))
        local_copy(staged[g].at[core], gathered[g].at[a, core], own_sem.at[g])

    def ring(g, half, first):
        axis_a = ROLES[g][0]
        a = at[axis_a]
        source = staged[g].at[half] if first else gathered[g].at[a, half]
        for way, by in enumerate((1, -1)):
            remote(source, gathered[g].at[a, half], a_send.at[g, way, half], a_recv.at[g, way, half], moved(at, axis_a, by))

    def spread_own(g, half, first):
        a = at[ROLES[g][0]]
        pair = a // 2
        source = staged[g].at[half] if first else gathered[g].at[a, half]
        remote(source, near[g].at[pair, a % 2, half], b_send.at[g, 0 if first else 4], b_recv.at[g, pair],
               moved(at, ROLES[g][1], 1 - 2 * pair))

    def spread(g, order, a_from):
        pair = a_from // 2
        remote(gathered[g].at[a_from], near[g].at[pair, a_from % 2], b_send.at[g, order], b_recv.at[g, pair],
               moved(at, ROLES[g][1], 1 - 2 * pair))

    for g in groups:
        ring(g, core, True)
    for g in groups:
        spread_own(g, core, True)
    code_box[...] = slot_codes(packed, placement)
    for g in groups:
        a = at[ROLES[g][0]]
        metas[g][a, core] = code_box[...]
        remote(code_box, metas[g].at[a, core], meta_send.at[g, 0], meta_recv.at[g, 0], moved(at, "x", 0, other))
    for g in groups:
        await_bytes(staged[g].at[0], core_recv.at[g])
        ring(g, other, False)
    for g in groups:
        spread_own(g, other, False)
    for g in groups:
        axis_a = ROLES[g][0]
        a = at[axis_a]
        await_bytes(code_box, meta_recv.at[g, 0])
        for by in (1, -1, 2):
            remote(metas[g].at[a], metas[g].at[a], meta_send.at[g, 1], meta_recv.at[g, 1], moved(at, axis_a, by))

    @pl.loop(0, 64)
    def _(unit):
        acc[pl.ds(pl.multiple_of(unit * UNIT, 8), UNIT), :] = jnp.zeros((UNIT, 2 * HID), jnp.float32)

    for way, by in enumerate((1, -1)):
        for g in groups:
            axis_a = ROLES[g][0]
            a_from = step_on(at[axis_a], -by)
            await_bytes(gathered[g].at[a_from, way], a_recv.at[g, way, way])
            remote(gathered[g].at[a_from, way], gathered[g].at[a_from, way], ah_send.at[g, way], ah_recv.at[g, way],
                   moved(at, axis_a, by))
    for way, by in enumerate((1, -1)):
        for g in groups:
            a_from = step_on(at[ROLES[g][0]], -by)
            await_bytes(gathered[g].at[a_from, 1 - way], a_recv.at[g, way, 1 - way])
            spread(g, 1 + way, a_from)
    for g in groups:
        await_bytes(metas[g].at[pl.ds(0, 3)], meta_recv.at[g, 1])
        for pair in range(2):
            remote(metas[g].at[pl.ds(2 * pair, 2)], near_metas[g].at[pair], meta_send.at[g, 2], meta_recv.at[g, 2],
                   moved(at, ROLES[g][1], 1 - 2 * pair))
    for g in groups:
        await_bytes(gathered[g].at[0, 0], own_sem.at[g])
        a_from = step_on(at[ROLES[g][0]], 2)
        for way in range(2):
            await_bytes(gathered[g].at[a_from, way], ah_recv.at[g, way])
        spread(g, 3, a_from)

    def line_base(g, by):
        _, axis_b, axis_c = ROLES[g]
        spot = dict(at)
        spot[axis_b] = step_on(at[axis_b], by)
        spot[axis_c] = 0
        spot["core"] = 0
        node, local = device(spot)
        return ((node * 8 + local) * SLOTS).astype(jnp.float32)

    def meta_of(g, is_near, pair, index, k):
        return near_metas[g][pair, index, k] if is_near else metas[g][pair * 2 + index, k]

    def slot_rows(g, is_near, pair, index, by):
        both = [meta_of(g, is_near, pair, index, k) for k in range(2)]
        table = jnp.concatenate(both, axis=1)
        first = lines[g] + line_base(g, by)
        slot = jnp.full((8, 2 * TOK), -100.0, jnp.float32)
        weight = jnp.zeros((8, 2 * TOK), jnp.float32)
        for k in range(TOPK):
            offset = table[k : k + 1] - first
            hit = jnp.logical_and(offset >= 0.0, offset < float(SLOTS))
            slot = jnp.where(hit, offset, slot)
            weight = jnp.where(hit, table[TOPK + k : TOPK + k + 1], weight)
        lane = lax.broadcasted_iota(jnp.int32, (8, 2 * TOK), 1)
        return slot + jnp.where(lane >= TOK, float(SLOTS), 0.0), weight

    def pick_and_send(g, kind):
        _, axis_b, axis_c = ROLES[g]
        is_near = kind >= 2

        @pl.loop(0, 2)
        def _(pair):
            if kind == 2:
                await_bytes(near[g].at[pair], b_recv.at[g, pair])
            ahead = 1 - 2 * pair
            by_b = (0, -ahead, 0, ahead)[kind]
            order = (0, 2 - pair, 1 + pair, 3)[kind]
            number = lax.broadcasted_iota(jnp.int32, (UNIT, 2 * TOK), 0).astype(jnp.float32)
            for i in range(2):
                slot, _ = slot_rows(g, is_near, pair, i, by_b)
                found = [jnp.where(number == slot[d : d + 1], 1.0, 0.0) for d in range(8)]
                share[0 : 8 * UNIT, i * 256 : (i + 1) * 256] = jnp.concatenate(found, axis=0).astype(jnp.bfloat16)
            for low_at, size in tiles(HALF[g]):
                span = slice(low_at, low_at + size)
                parts = []
                for i in range(2):
                    block = near[g][pair, i, :, :, span] if is_near else gathered[g][pair * 2 + i, :, :, span]
                    picked = jnp.dot(share[0 : 8 * UNIT, i * 256 : (i + 1) * 256], block.reshape(2 * TOK, size),
                                     preferred_element_type=jnp.float32)
                    parts.append(picked.reshape(8, UNIT, size))
                outbox[g][kind * 2 + pair, :, :, span] = jnp.concatenate(parts, axis=1).astype(jnp.bfloat16)
            c = at[axis_c]
            for by in (1, -1, 2, 0):
                c_to = step_on(c, by)
                for k in range(2):
                    core_to = (core + k) % 2
                    box = outbox[g].at[kind * 2 + pair, c_to * 2 + core_to]
                    slot = inbox[g].at[order, core, c, pair]
                    if by == 0 and k == 0 and kind in (0, 2):
                        local_copy(box, slot, row_recv.at[g, order])
                    else:
                        remote(box, slot, row_send.at[g, kind], row_recv.at[g, order],
                               moved(at, axis_c, by, core_to, axis_b, by_b))

    def bring(g, order):
        await_bytes(inbox[g].at[order], row_recv.at[g, order])
        for h in range(2):
            local_copy(inbox[g].at[order, h], stage.at[g % 2, :, :, :, pl.ds(h * HALF[g], HALF[g])], stage_sem.at[g % 2])

    def multiply(g, order):
        axis_a, axis_b, axis_c = ROLES[g]
        b_from = step_on(at[axis_b], STEPS[order])
        await_bytes(stage.at[g % 2, :, :, :, pl.ds(0, WIDTH[g])], stage_sem.at[g % 2])

        @pl.loop(0, 2)
        def _(tile):
            columns = pl.ds(pl.multiple_of(tile * HID, 256), HID)
            rows = stage[g % 2, :, :, :, 0 : WIDTH[g]].reshape(384, WIDTH[g])
            total = jnp.dot(rows, weights[START[g] : START[g] + WIDTH[g], columns], preferred_element_type=jnp.float32)
            for c in range(SIDE):
                for a in range(SIDE):
                    unit = a * STRIDE[axis_a] + b_from * STRIDE[axis_b] + c * STRIDE[axis_c]
                    low_at = (c * SIDE + a) * UNIT
                    acc[pl.ds(pl.multiple_of(unit * UNIT, 8), UNIT), columns] += total[low_at : low_at + UNIT]

    for kind in (0, 1):
        for g in groups:
            pick_and_send(g, kind)
    for g in groups:
        await_bytes(near_metas[g], meta_recv.at[g, 2])
    for kind in (2, 3):
        for g in groups:
            pick_and_send(g, kind)
    await_bytes(weights.at[:, pl.ds(0, HID)], w_sem.at[0])
    await_bytes(weights.at[:, pl.ds(HID, HID)], w_sem.at[1])

    def down_of(g):
        return weights.at[pl.ds(g * HID, HID), pl.ds(0, WIDTH[g])]

    def fetch_down(g):
        local_copy(down_w.at[0, :, pl.ds(START[g], WIDTH[g])], down_of(g), w_sem.at[2 + g])

    for order in (0, 1, 2, 3):
        bring(0, order)
        for g in groups:
            if g < 2:
                bring(g + 1, order)
            multiply(g, order)
            if order == 3 and g == 0:
                fetch_down(0)
                fetch_down(1)
            if order == 3 and g == 1:
                fetch_down(2)

    @pl.loop(0, 64)
    def _(unit):
        rows = pl.ds(pl.multiple_of(unit * UNIT, 8), UNIT)
        gate, up = acc[rows, 0:HID], acc[rows, HID : 2 * HID]
        hidden = gate / (1.0 + jnp.exp(-gate)) * up
        acc[rows, 0:HID] = hidden.astype(jnp.bfloat16).astype(jnp.float32)

    for g in groups:
        for kind in range(4):
            count = 7 if kind in (0, 2) else 8
            await_bytes(outbox[g].at[pl.ds(0, 2), pl.ds(0, count)], row_send.at[g, kind])
    for g in groups:
        await_bytes(down_of(g), w_sem.at[2 + g])

    def expand_and_send(g, order):
        axis_a, axis_b, axis_c = ROLES[g]
        b_to = step_on(at[axis_b], STEPS[order])
        for c in range(SIDE):
            units = [
                acc[pl.ds(pl.multiple_of(
                    (a * STRIDE[axis_a] + b_to * STRIDE[axis_b] + c * STRIDE[axis_c]) * UNIT, 8), UNIT), 0:HID]
                for a in range(SIDE)
            ]
            rows_bf[c * 96 : (c + 1) * 96, :] = jnp.concatenate(units, axis=0).astype(jnp.bfloat16)

        c = at[axis_c]
        for k in range(2):
            core_to = (core + k) % 2
            for low_at, size in tiles(HALF[g]):
                columns = pl.ds(pl.multiple_of(core_to * HALF[g] + low_at, 128), size)
                made = jnp.dot(rows_bf[...], weights[g * HID : (g + 1) * HID, columns], preferred_element_type=jnp.float32)
                made = made.astype(jnp.bfloat16).reshape(SIDE, 2, 48, size)
                for pair in range(2):
                    outbox[g][order * 2 + pair, pl.ds(core_to * SIDE, SIDE), :, low_at : low_at + size] = made[:, pair]
            for pair in range(2):
                kind, by_b = RETURNS[order, pair]
                for by in (1, -1, 2, 0):
                    c_to = step_on(c, by)
                    box = outbox[g].at[order * 2 + pair, core_to * SIDE + c_to]
                    slot = backbox[g].at[kind // 2, pair, kind % 2, c * 2 + core]
                    sem = back_recv.at[g, kind // 2, pair]
                    if by == 0 and k == 0 and by_b == 0:
                        local_copy(box, slot, sem)
                    else:
                        remote(box, slot, back_send.at[g, order, pair], sem, moved(at, axis_c, by, core_to, axis_b, by_b))

    def build_share(g, is_near, pair, target):
        ahead = 1 - 2 * pair
        number = lax.broadcasted_iota(jnp.int32, (48, 2 * TOK), 0).astype(jnp.float32)
        for side, by in enumerate((0, ahead if is_near else -ahead)):
            for i in range(2):
                slot, weight = slot_rows(g, is_near, pair, i, by)
                slot = slot + float(i * UNIT)
                found = [jnp.where(number == slot[d : d + 1], weight[d : d + 1], 0.0) for d in range(8)]
                ref, at_row, at_column = target
                total = jnp.concatenate(found, axis=0).T.astype(jnp.bfloat16)
                ref[at_row + i * 256 : at_row + (i + 1) * 256, pl.ds(at_column + side * 384, 384)] = total

    def home_share(g, pair):
        return weights, 3 * HID + g * 512, pl.multiple_of(pair * 768, 128)

    def combine(g, is_near, place):
        wide = pl.ds(0, HALF[g])
        views = lot.at[:, :, :, :, wide]
        for pair in range(2):
            await_bytes(backbox[g].at[int(is_near), pair], back_recv.at[g, int(is_near), pair])
            local_copy(backbox[g].at[int(is_near), pair], views.at[pair], stage_sem.at[pair])
            if not is_near:
                await_bytes(landed[g].at[pair], sum_recv.at[g, pair])
                local_copy(landed[g].at[pair], low.at[pair, :, :, :, wide], stage_sem.at[2 + pair])

        @pl.loop(0, 2)
        def _(pair):
            if is_near:
                build_share(g, True, pair, (share, 0, 0))
            await_bytes(views.at[pair], stage_sem.at[pair])
            if not is_near:
                await_bytes(low.at[pair, :, :, :, wide], stage_sem.at[2 + pair])
            for low_at, size in mix_tiles(HALF[g]):
                block = lot[pair, :, :, :, low_at : low_at + size].reshape(768, size)
                if is_near:
                    shares = share[...]
                else:
                    ref, at_row, at_column = home_share(g, pair)
                    shares = ref[at_row : at_row + 512, pl.ds(at_column, 768)]
                mixed = jnp.dot(shares, block, preferred_element_type=jnp.float32)
                place(pair, low_at, size, mixed.reshape(2, 2, TOK, size))

    def pass_on(g):
        def place(pair, low_at, size, block):
            near[g][pair, :, :, :, low_at : low_at + size] = block.astype(jnp.bfloat16)

        combine(g, True, place)
        for pair in range(2):
            remote(near[g].at[pair], landed[g].at[pair], sum_send.at[g, pair], sum_recv.at[g, pair],
                   moved(at, ROLES[g][1], 2 * pair - 1))

    def own_at(g, chip, half):
        rows = pl.ds(pl.multiple_of((chip * 2 + half) * TOK, TOK), TOK)
        if g == 2:
            return own2, rows, 0
        return acc, rows, g * WIDE

    def settled(g, chip, half):
        ref, rows, column = own_at(g, chip, half)
        return ref[rows, column : column + HALF[g]]

    def home(g):
        axis_a = ROLES[g][0]

        def place(pair, low_at, size, block):
            for i in range(2):
                for half in range(2):
                    ref, rows, column = own_at(g, pair * 2 + i, half)
                    value = block[i, half] + low[pair, i, half, :, low_at : low_at + size].astype(jnp.float32)
                    ref[rows, column + low_at : column + low_at + size] = value

        combine(g, False, place)
        opposite = step_on(at[axis_a], 2)
        for half, by in enumerate((1, -1)):
            gathered[g][0, half] = settled(g, opposite, half).astype(jnp.bfloat16)
            remote(gathered[g].at[0, half], arrived[g].at[half], c_send.at[g, half], c_recv.at[g, half],
                   moved(at, axis_a, by))
        for half_in, by in enumerate((1, -1)):
            half = 1 - half_in
            gathered[g][1 + half_in, half] = settled(g, step_on(at[axis_a], by), half).astype(jnp.bfloat16)
            pass_half(g, half_in, half, by)

    def pass_half(g, half_in, half, by):
        remote(gathered[g].at[1 + half_in, half], arrived[g].at[2 + 2 * half_in + half], c_send.at[g, 2 + half_in],
               c_recv.at[g, 2 + half_in], moved(at, ROLES[g][0], by))

    def relay(g):
        for half_in, by in enumerate((1, -1)):
            await_bytes(arrived[g].at[half_in], c_recv.at[g, half_in])
            value = settled(g, step_on(at[ROLES[g][0]], by), half_in) + arrived[g][half_in].astype(jnp.float32)
            gathered[g][1 + half_in, half_in] = value.astype(jnp.bfloat16)
            pass_half(g, half_in, half_in, by)

    def finish(g):
        for index in range(2):
            await_bytes(arrived[g].at[pl.ds(2 + 2 * index, 2)], c_recv.at[g, 2 + index])
        for half in range(2):
            value = settled(g, at[ROLES[g][0]], half) + arrived[g][2 + half].astype(jnp.float32)
            value = value + arrived[g][4 + half].astype(jnp.float32)
            last[half, :, START[g] // 2 : START[g] // 2 + HALF[g]] = value.astype(jnp.bfloat16)
        span = pl.ds(START[g] // 2, HALF[g])
        remote(last.at[other, :, span], ends[g], end_send.at[g], end_recv.at[g], moved(at, "x", 0, other))

    for order in (3, 1, 2, 0):
        for g in groups:
            expand_and_send(g, order)
    for g in groups:

        @pl.loop(0, 2)
        def _(pair):
            build_share(g, False, pair, home_share(g, pair))

    for g in groups:
        pass_on(g)
    for g in groups:
        for way in range(2):
            for half in range(2):
                await_bytes(gathered[g].at[0, 0], a_send.at[g, way, half])
            await_bytes(gathered[g].at[0, 0], ah_send.at[g, way])
        for order in range(5):
            await_bytes(gathered[g].at[0] if order in (1, 2, 3) else gathered[g].at[0, 0], b_send.at[g, order])
    home(0)
    home(1)
    relay(0)
    home(2)
    relay(1)
    relay(2)
    for g in groups:
        finish(g)
    for g in groups:
        mine = last[core, :, START[g] // 2 : START[g] // 2 + HALF[g]]
        await_bytes(ends[g], end_recv.at[g])
        theirs = ends[g][...]
        result[:, START[g] : START[g] + HALF[g]] = jnp.where(core == 0, mine, theirs)
        result[:, START[g] + HALF[g] : START[g] + WIDTH[g]] = jnp.where(core == 0, theirs, mine)
    for g in groups:
        await_bytes(metas[g].at[0, 0], meta_send.at[g, 0])
        await_bytes(metas[g].at[pl.ds(0, 3)], meta_send.at[g, 1])
        await_bytes(near_metas[g], meta_send.at[g, 2])
        await_bytes(staged[g].at[0], core_send.at[g])
        for order in range(4):
            for pair in range(2):
                count = 7 if RETURNS[order, pair][1] == 0 else 8
                await_bytes(outbox[g].at[0, pl.ds(0, count)], back_send.at[g, order, pair])
        for index in range(2):
            await_bytes(near[g].at[index], sum_send.at[g, index])
            await_bytes(arrived[g].at[index], c_send.at[g, index])
            await_bytes(arrived[g].at[pl.ds(0, 2)], c_send.at[g, 2 + index])
        await_bytes(ends[g], end_send.at[g])


def line_table():
    expert = np.arange(8)
    tables = []
    for roles in ROLES:
        spot = {"x": 0 * expert, "y": 0 * expert, "z": 0 * expert, "core": expert % 2}
        spot[roles[2]] = expert // 2
        node, local = device(spot)
        tables.append((node * 8 + local) * SLOTS)
    return jnp.asarray(np.stack(tables)[:, :, None].astype(np.float32))


def body(tokens, norm_gain, routes, route_gates, placement, gate_weight, up_weight, down_weight):
    bf16, f32 = jnp.bfloat16, jnp.float32
    packed = jnp.concatenate([routes.astype(f32), route_gates, jnp.zeros((TOK, TOK - 2 * TOPK), f32)], axis=1)

    vmem, hbm = pl.BlockSpec(memory_space=pltpu.VMEM), pl.BlockSpec(memory_space=pltpu.HBM)
    dma = pltpu.SemaphoreType.DMA
    shape = jax.ShapeDtypeStruct
    meta = (2, 2 * TOPK, TOK)

    def each(*dims):
        return [pltpu.VMEM((*dims, h), bf16) for h in HALF]

    result, *_ = pl.pallas_call(
        kernel,
        out_shape=[shape((TOK, D), bf16)]
        + [shape((4, 2, SIDE, 2, 48, h), bf16) for h in HALF]
        + [shape((2, 2, 2, 8, 48, h), bf16) for h in HALF]
        + [shape((2, 2, 2, TOK, h), bf16) for h in HALF],
        in_specs=[vmem] * 5 + [hbm] * 3,
        out_specs=[vmem] + [hbm] * 9,
        scratch_shapes=each(SIDE, 2, TOK)
        + each(2, 2, 2, TOK)
        + each(8, 8, 48)
        + each(2, TOK)
        + [pltpu.VMEM((SIDE, *meta), f32)] * 3
        + [pltpu.VMEM((2, 2, *meta), f32)] * 3
        + [
            pltpu.VMEM((2 * TOPK, TOK), f32),
            pltpu.VMEM((2, SIDE, 2, 48, 2 * WIDE), bf16),
            pltpu.VMEM((2, 2, 8, 48, WIDE), bf16),
            pltpu.VMEM((512, 768), bf16),
            pltpu.VMEM((384, HID), bf16),
            pltpu.VMEM((D, 2 * HID), bf16),
            pltpu.VMEM((64 * UNIT, 2 * HID), f32),
            pltpu.VMEM((SIDE * 2 * TOK, HALF[2]), f32),
            pltpu.VMEM((2, 2, 2, TOK, WIDE), bf16),
        ]
        + each(6, TOK)
        + [pltpu.VMEM((2, TOK, D // 2), bf16)]
        + each(TOK)
        + [
            dma((5,)), dma((3,)), dma((3,)), dma((3,)), dma((3, 3)), dma((3, 3)),
            dma((3, 2, 2)), dma((3, 2, 2)), dma((3, 2)), dma((3, 2)), dma((3, 5)), dma((3, 2)),
            dma((3, 4)), dma((3, 4)), dma((4,)), dma((3, 4, 2)), dma((3, 2, 2)), dma((3, 2)), dma((3, 2)),
            dma((3, 4)), dma((3, 4)), dma((3,)), dma((3,)),
        ],
        compiler_params=pltpu.CompilerParams(collective_id=0, has_side_effects=True, vmem_limit_bytes=VMEM_LIMIT),
        name="experts",
    )(tokens, norm_gain[None, :], packed, placement[None, :], line_table(), gate_weight, up_weight, down_weight)
    return result


def solution(mesh):
    rows = P(("node", "local"), None)
    whole = P(("node", "local"), None, None)
    in_specs = (rows, P(), rows, rows, P(), whole, whole, whole)
    return jax.shard_map(body, mesh=mesh, in_specs=in_specs, out_specs=rows, check_vma=False)
```

```python
import jax
import jax.numpy as jnp
import numpy as np
from jax import lax
from jax.experimental import pallas as pl
from jax.experimental.pallas import tpu as pltpu
from jax.sharding import PartitionSpec as P

MESH = pl.DeviceIdType.MESH
BLOCK_TOK = 32
CAP = 3
EPSILON = 1e-06
SIDE = 4
TOK = 128
TOPK = 8
D = 4096
HID = 768
SLOTS = 12
UNIT = 2 * SLOTS
ROLES = (("x", "y", "z"), ("y", "z", "x"), ("z", "x", "y"))
WIDTH = (1536, 1280, 1280)
START = (0, 1536, 2816)
HALF = tuple(w // 2 for w in WIDTH)
WIDE = max(HALF)
STRIDE = {"x": 16, "y": 4, "z": 1}
STEPS = (0, -1, 1, 2)
RETURNS = {
    (0, 0): (0, 0), (0, 1): (0, 0),
    (1, 0): (2, 0), (1, 1): (1, -1),
    (2, 0): (1, 1), (2, 1): (2, 0),
    (3, 0): (3, -1), (3, 1): (3, 1),
}
VMEM_LIMIT = 62 << 20
MIX = 768
EXP = 768


def position():
    node, local = lax.axis_index("node"), lax.axis_index("local")
    return {
        "x": (node // 2) % 2 * 2 + local % 2,
        "y": node // 4,
        "z": local // 2,
        "core": node % 2,
    }


def device(at):
    node = (at["y"] * 2 + at["x"] // 2) * 2 + at["core"]
    return node, at["z"] * 2 + at["x"] % 2


def step_on(value, by):
    return (value + by + SIDE) % SIDE


def moved(at, axis, by, core=None, axis2=None, by2=0):
    new = dict(at)
    new[axis] = step_on(at[axis], by)
    if axis2 is not None:
        new[axis2] = step_on(at[axis2], by2)
    if core is not None:
        new["core"] = core
    return device(new)


def greet(at, barrier):
    other = 1 - at["core"]
    partners = [moved(at, "x", 0, other)]
    for _, axis_b, axis_c in ROLES:
        for by in (1, -1, 2):
            for core in (at["core"], other):
                partners.append(moved(at, axis_c, by, core))
                for side in (1, -1):
                    partners.append(moved(at, axis_c, by, core, axis_b, side))
    for partner in partners:
        pl.semaphore_signal(barrier, inc=1, device_id=partner, device_id_type=MESH)
    return len(partners)


def remote(src, dst, send, recv, target):
    pltpu.make_async_remote_copy(
        src_ref=src, dst_ref=dst, send_sem=send, recv_sem=recv, device_id=target, device_id_type=MESH
    ).start()


def local_copy(src, dst, sem):
    pltpu.make_async_copy(src, dst, sem).start()


def await_bytes(ref, sem):
    pltpu.make_async_copy(ref, ref, sem).wait()


def mix_tiles(width):
    return [(at, min(MIX, width - at)) for at in range(0, width, MIX)]


def tiles(width):
    return [(at, min(EXP, width - at)) for at in range(0, width, EXP)]


def slot_codes(packed, placement):
    side = (TOK, TOK)
    down = lax.broadcasted_iota(jnp.int32, side, 0)
    across = lax.broadcasted_iota(jnp.int32, side, 1)
    earlier = jnp.logical_and(down < across, down // BLOCK_TOK == across // BLOCK_TOK)
    place = jnp.broadcast_to(placement[...].astype(jnp.float32), side).T
    index = down.astype(jnp.float32)
    columns = [jnp.broadcast_to(packed[:, k : k + 1], side) for k in range(TOPK)]
    table = packed[...].T
    block = (across[0:1] // BLOCK_TOK * CAP).astype(jnp.float32)
    codes = []
    for k in range(TOPK):
        wanted = table[k : k + 1]
        holder = jnp.sum(jnp.where(place == wanted, index, 0.0), axis=0, keepdims=True)
        same = columns[0] == wanted
        for column in columns[1:]:
            same = jnp.logical_or(same, column == wanted)
        count = jnp.sum(jnp.where(jnp.logical_and(same, earlier), 1.0, 0.0), axis=0, keepdims=True)
        codes.append(holder * float(SLOTS) + block + count)
    gates = table[TOPK : 2 * TOPK]
    weight = gates / jnp.sum(gates, axis=0, keepdims=True)
    return jnp.concatenate(codes + [weight.astype(jnp.bfloat16).astype(jnp.float32)], axis=0)


def kernel(
    tokens, gain, packed, placement, lines, gate_w, up_w, down_w,
    result, in0, in1, in2, back0, back1, back2, land0, land1, land2,
    g0, g1, g2, n0, n1, n2, out0, out1, out2, st0, st1, st2, m0, m1, m2, k0, k1, k2,
    code_box, stage, lot, share, rows_bf, weights, acc, own2, low, r0, r1, r2, last, end0, end1, end2,
    w_sem, own_sem, core_send, core_recv, meta_send, meta_recv, a_send, a_recv, ah_send, ah_recv, b_send, b_recv,
    row_send, row_recv, stage_sem, back_send, back_recv, sum_send, sum_recv, c_send, c_recv, end_send, end_recv,
):
    at = position()
    core = at["core"]
    other = 1 - core
    groups = range(3)
    gathered, near, outbox, inbox = (g0, g1, g2), (n0, n1, n2), (out0, out1, out2), (in0, in1, in2)
    staged, metas, near_metas = (st0, st1, st2), (m0, m1, m2), (k0, k1, k2)
    backbox, landed, arrived, ends = (back0, back1, back2), (land0, land1, land2), (r0, r1, r2), (end0, end1, end2)
    barrier = pltpu.get_barrier_semaphore()
    greeted = greet(at, barrier)
    local_copy(gate_w.at[0], weights.at[:, pl.ds(0, HID)], w_sem.at[0])
    local_copy(up_w.at[0], weights.at[:, pl.ds(HID, HID)], w_sem.at[1])

    @pl.loop(0, TOK // 16)
    def _(step):
        rows = pl.ds(pl.multiple_of(step * 16, 16), 16)
        values = tokens[rows, :].astype(jnp.float32)
        rescale = lax.rsqrt(jnp.sum(values * values, axis=-1, keepdims=True) * (1.0 / D) + EPSILON)
        normed = (values * rescale * gain[...].astype(jnp.float32)).astype(jnp.bfloat16)
        for g in groups:
            for h in range(2):
                low_at = START[g] + h * HALF[g]
                staged[g][h, rows, :] = normed[:, low_at : low_at + HALF[g]]

    pl.semaphore_wait(barrier, greeted)
    for g in groups:
        a = at[ROLES[g][0]]
        remote(staged[g].at[other], gathered[g].at[a, core], core_send.at[g], core_recv.at[g], moved(at, "x", 0, other))
        local_copy(staged[g].at[core], gathered[g].at[a, core], own_sem.at[g])

    def ring(g, half, first):
        axis_a = ROLES[g][0]
        a = at[axis_a]
        source = staged[g].at[half] if first else gathered[g].at[a, half]
        for way, by in enumerate((1, -1)):
            remote(source, gathered[g].at[a, half], a_send.at[g, way, half], a_recv.at[g, way, half], moved(at, axis_a, by))

    def spread_own(g, half, first):
        a = at[ROLES[g][0]]
        pair = a // 2
        source = staged[g].at[half] if first else gathered[g].at[a, half]
        remote(source, near[g].at[pair, a % 2, half], b_send.at[g, 0 if first else 4], b_recv.at[g, pair],
               moved(at, ROLES[g][1], 1 - 2 * pair))

    def spread(g, order, a_from):
        pair = a_from // 2
        remote(gathered[g].at[a_from], near[g].at[pair, a_from % 2], b_send.at[g, order], b_recv.at[g, pair],
               moved(at, ROLES[g][1], 1 - 2 * pair))

    for g in groups:
        ring(g, core, True)
    for g in groups:
        spread_own(g, core, True)
    code_box[...] = slot_codes(packed, placement)
    for g in groups:
        a = at[ROLES[g][0]]
        metas[g][a, core] = code_box[...]
        remote(code_box, metas[g].at[a, core], meta_send.at[g, 0], meta_recv.at[g, 0], moved(at, "x", 0, other))
    for g in groups:
        await_bytes(staged[g].at[0], core_recv.at[g])
        ring(g, other, False)
    for g in groups:
        spread_own(g, other, False)
    for g in groups:
        axis_a = ROLES[g][0]
        a = at[axis_a]
        await_bytes(code_box, meta_recv.at[g, 0])
        for by in (1, -1, 2):
            remote(metas[g].at[a], metas[g].at[a], meta_send.at[g, 1], meta_recv.at[g, 1], moved(at, axis_a, by))

    @pl.loop(0, 64)
    def _(unit):
        acc[pl.ds(pl.multiple_of(unit * UNIT, 8), UNIT), :] = jnp.zeros((UNIT, 2 * HID), jnp.float32)

    for way, by in enumerate((1, -1)):
        for g in groups:
            axis_a = ROLES[g][0]
            a_from = step_on(at[axis_a], -by)
            await_bytes(gathered[g].at[a_from, way], a_recv.at[g, way, way])
            remote(gathered[g].at[a_from, way], gathered[g].at[a_from, way], ah_send.at[g, way], ah_recv.at[g, way],
                   moved(at, axis_a, by))
    for way, by in enumerate((1, -1)):
        for g in groups:
            a_from = step_on(at[ROLES[g][0]], -by)
            await_bytes(gathered[g].at[a_from, 1 - way], a_recv.at[g, way, 1 - way])
            spread(g, 1 + way, a_from)
    for g in groups:
        await_bytes(metas[g].at[pl.ds(0, 3)], meta_recv.at[g, 1])
        for pair in range(2):
            remote(metas[g].at[pl.ds(2 * pair, 2)], near_metas[g].at[pair], meta_send.at[g, 2], meta_recv.at[g, 2],
                   moved(at, ROLES[g][1], 1 - 2 * pair))
    for g in groups:
        await_bytes(gathered[g].at[0, 0], own_sem.at[g])
        a_from = step_on(at[ROLES[g][0]], 2)
        for way in range(2):
            await_bytes(gathered[g].at[a_from, way], ah_recv.at[g, way])
        spread(g, 3, a_from)

    def line_base(g, by):
        _, axis_b, axis_c = ROLES[g]
        spot = dict(at)
        spot[axis_b] = step_on(at[axis_b], by)
        spot[axis_c] = 0
        spot["core"] = 0
        node, local = device(spot)
        return ((node * 8 + local) * SLOTS).astype(jnp.float32)

    def meta_of(g, is_near, pair, index, k):
        return near_metas[g][pair, index, k] if is_near else metas[g][pair * 2 + index, k]

    def slot_rows(g, is_near, pair, index, by):
        both = [meta_of(g, is_near, pair, index, k) for k in range(2)]
        table = jnp.concatenate(both, axis=1)
        first = lines[g] + line_base(g, by)
        slot = jnp.full((8, 2 * TOK), -100.0, jnp.float32)
        weight = jnp.zeros((8, 2 * TOK), jnp.float32)
        for k in range(TOPK):
            offset = table[k : k + 1] - first
            hit = jnp.logical_and(offset >= 0.0, offset < float(SLOTS))
            slot = jnp.where(hit, offset, slot)
            weight = jnp.where(hit, table[TOPK + k : TOPK + k + 1], weight)
        lane = lax.broadcasted_iota(jnp.int32, (8, 2 * TOK), 1)
        return slot + jnp.where(lane >= TOK, float(SLOTS), 0.0), weight

    def pick_and_send(g, kind):
        _, axis_b, axis_c = ROLES[g]
        is_near = kind >= 2

        @pl.loop(0, 2)
        def _(pair):
            if kind == 2:
                await_bytes(near[g].at[pair], b_recv.at[g, pair])
            ahead = 1 - 2 * pair
            by_b = (0, -ahead, 0, ahead)[kind]
            order = (0, 2 - pair, 1 + pair, 3)[kind]
            number = lax.broadcasted_iota(jnp.int32, (UNIT, 2 * TOK), 0).astype(jnp.float32)
            for i in range(2):
                slot, _ = slot_rows(g, is_near, pair, i, by_b)
                found = [jnp.where(number == slot[d : d + 1], 1.0, 0.0) for d in range(8)]
                share[0 : 8 * UNIT, i * 256 : (i + 1) * 256] = jnp.concatenate(found, axis=0).astype(jnp.bfloat16)
            for low_at, size in tiles(HALF[g]):
                span = slice(low_at, low_at + size)
                parts = []
                for i in range(2):
                    block = near[g][pair, i, :, :, span] if is_near else gathered[g][pair * 2 + i, :, :, span]
                    picked = jnp.dot(share[0 : 8 * UNIT, i * 256 : (i + 1) * 256], block.reshape(2 * TOK, size),
                                     preferred_element_type=jnp.float32)
                    parts.append(picked.reshape(8, UNIT, size))
                outbox[g][kind * 2 + pair, :, :, span] = jnp.concatenate(parts, axis=1).astype(jnp.bfloat16)
            c = at[axis_c]
            for by in (1, -1, 2, 0):
                c_to = step_on(c, by)
                for k in range(2):
                    core_to = (core + k) % 2
                    box = outbox[g].at[kind * 2 + pair, c_to * 2 + core_to]
                    slot = inbox[g].at[order, core, c, pair]
                    if by == 0 and k == 0 and kind in (0, 2):
                        local_copy(box, slot, row_recv.at[g, order])
                    else:
                        remote(box, slot, row_send.at[g, kind], row_recv.at[g, order],
                               moved(at, axis_c, by, core_to, axis_b, by_b))

    def bring(g, order):
        await_bytes(inbox[g].at[order], row_recv.at[g, order])
        for h in range(2):
            local_copy(inbox[g].at[order, h], stage.at[g % 2, :, :, :, pl.ds(h * HALF[g], HALF[g])], stage_sem.at[g % 2])

    def multiply(g, order):
        axis_a, axis_b, axis_c = ROLES[g]
        b_from = step_on(at[axis_b], STEPS[order])
        await_bytes(stage.at[g % 2, :, :, :, pl.ds(0, WIDTH[g])], stage_sem.at[g % 2])

        @pl.loop(0, 2)
        def _(tile):
            columns = pl.ds(pl.multiple_of(tile * HID, 256), HID)
            rows = stage[g % 2, :, :, :, 0 : WIDTH[g]].reshape(384, WIDTH[g])
            total = jnp.dot(rows, weights[START[g] : START[g] + WIDTH[g], columns], preferred_element_type=jnp.float32)
            for c in range(SIDE):
                for a in range(SIDE):
                    unit = a * STRIDE[axis_a] + b_from * STRIDE[axis_b] + c * STRIDE[axis_c]
                    low_at = (c * SIDE + a) * UNIT
                    acc[pl.ds(pl.multiple_of(unit * UNIT, 8), UNIT), columns] += total[low_at : low_at + UNIT]

    for kind in (0, 1):
        for g in groups:
            pick_and_send(g, kind)
    for g in groups:
        await_bytes(near_metas[g], meta_recv.at[g, 2])
    for kind in (2, 3):
        for g in groups:
            pick_and_send(g, kind)
    await_bytes(weights.at[:, pl.ds(0, HID)], w_sem.at[0])
    await_bytes(weights.at[:, pl.ds(HID, HID)], w_sem.at[1])

    def down_of(g):
        return weights.at[pl.ds(g * HID, HID), pl.ds(0, WIDTH[g])]

    def fetch_down(g):
        local_copy(down_w.at[0, :, pl.ds(START[g], WIDTH[g])], down_of(g), w_sem.at[2 + g])

    for order in (0, 1, 2, 3):
        bring(0, order)
        for g in groups:
            if g < 2:
                bring(g + 1, order)
            multiply(g, order)
            if order == 3 and g == 0:
                fetch_down(0)
                fetch_down(1)
            if order == 3 and g == 1:
                fetch_down(2)

    @pl.loop(0, 64)
    def _(unit):
        rows = pl.ds(pl.multiple_of(unit * UNIT, 8), UNIT)
        gate, up = acc[rows, 0:HID], acc[rows, HID : 2 * HID]
        hidden = gate / (1.0 + jnp.exp(-gate)) * up
        acc[rows, 0:HID] = hidden.astype(jnp.bfloat16).astype(jnp.float32)

    for g in groups:
        for kind in range(4):
            count = 7 if kind in (0, 2) else 8
            await_bytes(outbox[g].at[pl.ds(0, 2), pl.ds(0, count)], row_send.at[g, kind])
    for g in groups:
        await_bytes(down_of(g), w_sem.at[2 + g])

    def expand_and_send(g, order):
        axis_a, axis_b, axis_c = ROLES[g]
        b_to = step_on(at[axis_b], STEPS[order])
        for c in range(SIDE):
            units = [
                acc[pl.ds(pl.multiple_of(
                    (a * STRIDE[axis_a] + b_to * STRIDE[axis_b] + c * STRIDE[axis_c]) * UNIT, 8), UNIT), 0:HID]
                for a in range(SIDE)
            ]
            rows_bf[c * 96 : (c + 1) * 96, :] = jnp.concatenate(units, axis=0).astype(jnp.bfloat16)

        for k in range(2):
            core_to = (core + k) % 2
            for low_at, size in tiles(HALF[g]):
                columns = pl.ds(pl.multiple_of(core_to * HALF[g] + low_at, 128), size)
                made = jnp.dot(rows_bf[...], weights[g * HID : (g + 1) * HID, columns], preferred_element_type=jnp.float32)
                made = made.astype(jnp.bfloat16).reshape(SIDE, 2, 48, size)
                for pair in range(2):
                    outbox[g][order * 2 + pair, pl.ds(core_to * SIDE, SIDE), :, low_at : low_at + size] = made[:, pair]
            for pair in range(2):
                if RETURNS[order, pair][0] != 1:
                    send_back(g, order, pair, k)

    def send_back(g, order, pair, k):
        _, axis_b, axis_c = ROLES[g]
        c = at[axis_c]
        core_to = (core + k) % 2
        kind, by_b = RETURNS[order, pair]
        for by in (1, -1, 2, 0):
            c_to = step_on(c, by)
            box = outbox[g].at[order * 2 + pair, core_to * SIDE + c_to]
            slot = backbox[g].at[kind // 2, pair, kind % 2, c * 2 + core]
            sem = back_recv.at[g, kind // 2, pair]
            if by == 0 and k == 0 and by_b == 0:
                local_copy(box, slot, sem)
            else:
                remote(box, slot, back_send.at[g, order, pair], sem, moved(at, axis_c, by, core_to, axis_b, by_b))

    def build_share(g, is_near, pair, target):
        ahead = 1 - 2 * pair
        number = lax.broadcasted_iota(jnp.int32, (48, 2 * TOK), 0).astype(jnp.float32)
        for side, by in enumerate((0, ahead if is_near else -ahead)):
            for i in range(2):
                slot, weight = slot_rows(g, is_near, pair, i, by)
                slot = slot + float(i * UNIT)
                found = [jnp.where(number == slot[d : d + 1], weight[d : d + 1], 0.0) for d in range(8)]
                ref, at_row, at_column = target
                total = jnp.concatenate(found, axis=0).T.astype(jnp.bfloat16)
                ref[at_row + i * 256 : at_row + (i + 1) * 256, pl.ds(at_column + side * 384, 384)] = total

    def home_share(g, pair):
        return weights, 3 * HID + g * 512, pl.multiple_of(pair * 768, 128)

    def combine(g, is_near, place):
        wide = pl.ds(0, HALF[g])
        views = lot.at[:, :, :, :, wide]
        for pair in range(2):
            await_bytes(backbox[g].at[int(is_near), pair], back_recv.at[g, int(is_near), pair])
            local_copy(backbox[g].at[int(is_near), pair], views.at[pair], stage_sem.at[pair])
            if not is_near:
                await_bytes(landed[g].at[pair], sum_recv.at[g, pair])
                local_copy(landed[g].at[pair], low.at[pair, :, :, :, wide], stage_sem.at[2 + pair])

        @pl.loop(0, 2)
        def _(pair):
            if is_near:
                build_share(g, True, pair, (share, 0, 0))
            await_bytes(views.at[pair], stage_sem.at[pair])
            if not is_near:
                await_bytes(low.at[pair, :, :, :, wide], stage_sem.at[2 + pair])
            for low_at, size in mix_tiles(HALF[g]):
                block = lot[pair, :, :, :, low_at : low_at + size].reshape(768, size)
                if is_near:
                    shares = share[...]
                else:
                    ref, at_row, at_column = home_share(g, pair)
                    shares = ref[at_row : at_row + 512, pl.ds(at_column, 768)]
                mixed = jnp.dot(shares, block, preferred_element_type=jnp.float32)
                place(pair, low_at, size, mixed.reshape(2, 2, TOK, size))

    def pass_on(g):
        def place(pair, low_at, size, block):
            near[g][pair, :, :, :, low_at : low_at + size] = block.astype(jnp.bfloat16)

        combine(g, True, place)
        for pair in range(2):
            remote(near[g].at[pair], landed[g].at[pair], sum_send.at[g, pair], sum_recv.at[g, pair],
                   moved(at, ROLES[g][1], 2 * pair - 1))

    def own_at(g, chip, half):
        rows = pl.ds(pl.multiple_of((chip * 2 + half) * TOK, TOK), TOK)
        if g == 2:
            return own2, rows, 0
        return acc, rows, g * WIDE

    def settled(g, chip, half):
        ref, rows, column = own_at(g, chip, half)
        return ref[rows, column : column + HALF[g]]

    def home(g):
        axis_a = ROLES[g][0]

        def place(pair, low_at, size, block):
            for i in range(2):
                for half in range(2):
                    ref, rows, column = own_at(g, pair * 2 + i, half)
                    value = block[i, half] + low[pair, i, half, :, low_at : low_at + size].astype(jnp.float32)
                    ref[rows, column + low_at : column + low_at + size] = value

        combine(g, False, place)
        opposite = step_on(at[axis_a], 2)
        for half, by in enumerate((1, -1)):
            gathered[g][0, half] = settled(g, opposite, half).astype(jnp.bfloat16)
            remote(gathered[g].at[0, half], arrived[g].at[half], c_send.at[g, half], c_recv.at[g, half],
                   moved(at, axis_a, by))
        for half_in, by in enumerate((1, -1)):
            half = 1 - half_in
            gathered[g][1 + half_in, half] = settled(g, step_on(at[axis_a], by), half).astype(jnp.bfloat16)
            pass_half(g, half_in, half, by)

    def pass_half(g, half_in, half, by):
        remote(gathered[g].at[1 + half_in, half], arrived[g].at[2 + 2 * half_in + half], c_send.at[g, 2 + half_in],
               c_recv.at[g, 2 + half_in], moved(at, ROLES[g][0], by))

    def relay(g):
        for half_in, by in enumerate((1, -1)):
            await_bytes(arrived[g].at[half_in], c_recv.at[g, half_in])
            value = settled(g, step_on(at[ROLES[g][0]], by), half_in) + arrived[g][half_in].astype(jnp.float32)
            gathered[g][1 + half_in, half_in] = value.astype(jnp.bfloat16)
            pass_half(g, half_in, half_in, by)

    def finish(g):
        for index in range(2):
            await_bytes(arrived[g].at[pl.ds(2 + 2 * index, 2)], c_recv.at[g, 2 + index])
        for half in range(2):
            value = settled(g, at[ROLES[g][0]], half) + arrived[g][2 + half].astype(jnp.float32)
            value = value + arrived[g][4 + half].astype(jnp.float32)
            last[half, :, START[g] // 2 : START[g] // 2 + HALF[g]] = value.astype(jnp.bfloat16)
        span = pl.ds(START[g] // 2, HALF[g])
        remote(last.at[other, :, span], ends[g], end_send.at[g], end_recv.at[g], moved(at, "x", 0, other))

    for order in (3, 1, 2):
        for g in groups:
            expand_and_send(g, order)
    for g in groups:

        @pl.loop(0, 2)
        def _(pair):
            build_share(g, False, pair, home_share(g, pair))

    for g in groups:
        for k in range(2):
            send_back(g, 1, 1, k)
            send_back(g, 2, 0, k)
    for g in groups:
        pass_on(g)
        expand_and_send(g, 0)
    for g in groups:
        for way in range(2):
            for half in range(2):
                await_bytes(gathered[g].at[0, 0], a_send.at[g, way, half])
            await_bytes(gathered[g].at[0, 0], ah_send.at[g, way])
        for order in range(5):
            await_bytes(gathered[g].at[0] if order in (1, 2, 3) else gathered[g].at[0, 0], b_send.at[g, order])
    home(0)
    home(1)
    relay(0)
    home(2)
    relay(1)
    relay(2)
    for g in groups:
        finish(g)
    for g in groups:
        mine = last[core, :, START[g] // 2 : START[g] // 2 + HALF[g]]
        await_bytes(ends[g], end_recv.at[g])
        theirs = ends[g][...]
        result[:, START[g] : START[g] + HALF[g]] = jnp.where(core == 0, mine, theirs)
        result[:, START[g] + HALF[g] : START[g] + WIDTH[g]] = jnp.where(core == 0, theirs, mine)
    for g in groups:
        await_bytes(metas[g].at[0, 0], meta_send.at[g, 0])
        await_bytes(metas[g].at[pl.ds(0, 3)], meta_send.at[g, 1])
        await_bytes(near_metas[g], meta_send.at[g, 2])
        await_bytes(staged[g].at[0], core_send.at[g])
        for order in range(4):
            for pair in range(2):
                count = 7 if RETURNS[order, pair][1] == 0 else 8
                await_bytes(outbox[g].at[0, pl.ds(0, count)], back_send.at[g, order, pair])
        for index in range(2):
            await_bytes(near[g].at[index], sum_send.at[g, index])
            await_bytes(arrived[g].at[index], c_send.at[g, index])
            await_bytes(arrived[g].at[pl.ds(0, 2)], c_send.at[g, 2 + index])
        await_bytes(ends[g], end_send.at[g])


def line_table():
    expert = np.arange(8)
    tables = []
    for roles in ROLES:
        spot = {"x": 0 * expert, "y": 0 * expert, "z": 0 * expert, "core": expert % 2}
        spot[roles[2]] = expert // 2
        node, local = device(spot)
        tables.append((node * 8 + local) * SLOTS)
    return jnp.asarray(np.stack(tables)[:, :, None].astype(np.float32))


def body(tokens, norm_gain, routes, route_gates, placement, gate_weight, up_weight, down_weight):
    bf16, f32 = jnp.bfloat16, jnp.float32
    packed = jnp.concatenate([routes.astype(f32), route_gates, jnp.zeros((TOK, TOK - 2 * TOPK), f32)], axis=1)

    vmem, hbm = pl.BlockSpec(memory_space=pltpu.VMEM), pl.BlockSpec(memory_space=pltpu.HBM)
    dma = pltpu.SemaphoreType.DMA
    shape = jax.ShapeDtypeStruct
    meta = (2, 2 * TOPK, TOK)

    def each(*dims):
        return [pltpu.VMEM((*dims, h), bf16) for h in HALF]

    result, *_ = pl.pallas_call(
        kernel,
        out_shape=[shape((TOK, D), bf16)]
        + [shape((4, 2, SIDE, 2, 48, h), bf16) for h in HALF]
        + [shape((2, 2, 2, 8, 48, h), bf16) for h in HALF]
        + [shape((2, 2, 2, TOK, h), bf16) for h in HALF],
        in_specs=[vmem] * 5 + [hbm] * 3,
        out_specs=[vmem] + [hbm] * 9,
        scratch_shapes=each(SIDE, 2, TOK)
        + each(2, 2, 2, TOK)
        + each(8, 8, 48)
        + each(2, TOK)
        + [pltpu.VMEM((SIDE, *meta), f32)] * 3
        + [pltpu.VMEM((2, 2, *meta), f32)] * 3
        + [
            pltpu.VMEM((2 * TOPK, TOK), f32),
            pltpu.VMEM((2, SIDE, 2, 48, 2 * WIDE), bf16),
            pltpu.VMEM((2, 2, 8, 48, WIDE), bf16),
            pltpu.VMEM((512, 768), bf16),
            pltpu.VMEM((384, HID), bf16),
            pltpu.VMEM((D, 2 * HID), bf16),
            pltpu.VMEM((64 * UNIT, 2 * HID), f32),
            pltpu.VMEM((SIDE * 2 * TOK, HALF[2]), f32),
            pltpu.VMEM((2, 2, 2, TOK, WIDE), bf16),
        ]
        + each(6, TOK)
        + [pltpu.VMEM((2, TOK, D // 2), bf16)]
        + each(TOK)
        + [
            dma((5,)), dma((3,)), dma((3,)), dma((3,)), dma((3, 3)), dma((3, 3)),
            dma((3, 2, 2)), dma((3, 2, 2)), dma((3, 2)), dma((3, 2)), dma((3, 5)), dma((3, 2)),
            dma((3, 4)), dma((3, 4)), dma((4,)), dma((3, 4, 2)), dma((3, 2, 2)), dma((3, 2)), dma((3, 2)),
            dma((3, 4)), dma((3, 4)), dma((3,)), dma((3,)),
        ],
        compiler_params=pltpu.CompilerParams(collective_id=0, has_side_effects=True, vmem_limit_bytes=VMEM_LIMIT),
        name="experts",
    )(tokens, norm_gain[None, :], packed, placement[None, :], line_table(), gate_weight, up_weight, down_weight)
    return result


def solution(mesh):
    rows = P(("node", "local"), None)
    whole = P(("node", "local"), None, None)
    in_specs = (rows, P(), rows, rows, P(), whole, whole, whole)
    return jax.shard_map(body, mesh=mesh, in_specs=in_specs, out_specs=rows, check_vma=False)
```
